32 devices in a mesh: frames: 2 (over y), codebook: 4 (over x, core), hidden: 4 (over z).
Axes of the slice: x: 2, y: 2, z: 4, core: 2. Of those that a mesh axis runs over, the one named last changes fastest.
Arguments:
- temporal: bfloat16 [1024, 4096], P(('frames', 'codebook'), 'hidden'), may hold values from -6 to 6
- frame_ids: int32 [1024, 4], P('frames', 'codebook'), may hold values from 0 to 2047
- proj_weight: bfloat16 [4, 4096, 1024], P('codebook', 'hidden'), may hold values from -0.09375 to 0.09375
- embed_table: bfloat16 [4, 2049, 1024], P('codebook'), may hold values from -6 to 6
- qkv_weight: bfloat16 [4, 3, 1024, 1024], P('codebook', None, None, 'hidden'), may hold values from -12 to 12
- out_weight: bfloat16 [4, 1024, 1024], P('codebook', 'hidden'), may hold values from -0.1875 to 0.1875
- gate_up: bfloat16 [4, 2, 1024, 4096], P('codebook', None, None, 'hidden'), may hold values from -0.1875 to 0.1875
- down_weight: bfloat16 [4, 4096, 1024], P('codebook', 'hidden'), may hold values from -0.09375 to 0.09375
- norm_gains: float32 [4, 2, 1024], P('codebook'), may hold values from 0.25 to 1.75
Outputs:
- depth_states: float32 [4, 1024, 1024], P('codebook', 'frames', 'hidden')
The draws below stay inside these ranges and needn't reach their ends.
All inputs are finite; a program needn't handle non-finite values.
Results may differ from the reference program's by a relative error of at most 0.015.
Values may be sent and summed in bfloat16 or wider, within the bound.
No kernel may reach another device: no remote copies, remote signals or barrier semaphores. Data moves between devices by JAX's collectives and lax.ppermute only.
A program may use at most 192 MiB of HBM per device.

```python
import math
import jax
import jax.numpy as jnp
from jax import lax

D = 4096
DD = 1024
HEADS = 16
HID = 4096
CARD = 2048
CODEBOOKS = 4
FRAMES = 1024


def draw_qkv_weight(key, part):
    base_key = jax.random.fold_in(key, 31)
    subkeys = jax.random.split(base_key, 5)
    base = jax.random.truncated_normal(subkeys[0], -4.0, 4.0, (CODEBOOKS, 3, DD, DD), jnp.float32) * DD ** (-0.5)
    chosen = jax.random.bernoulli(subkeys[1], 0.125, (CODEBOOKS, HEADS))
    first_book = jax.random.randint(subkeys[2], (), 0, CODEBOOKS)
    first_head = jax.random.randint(subkeys[3], (), 0, HEADS)
    forced = (jnp.arange(CODEBOOKS)[:, None] == first_book) & (jnp.arange(HEADS)[None, :] == first_head)
    chosen = chosen | forced
    lowest = 0.25
    spread = jax.random.uniform(subkeys[4], (CODEBOOKS, HEADS), jnp.float32, math.log(lowest), math.log(3.0))
    strength = jnp.exp(spread) * DD ** 0.5
    column_strength = jnp.repeat(strength, DD // HEADS, axis=1)
    column_chosen = jnp.repeat(chosen, DD // HEADS, axis=1)
    query_part = jnp.where(column_chosen[:, None, :], column_strength[:, None, :] * base[:, 1], base[:, 0])
    query_part = jnp.clip(query_part, -12.0, 12.0)
    return jnp.stack([query_part, base[:, 1], base[:, 2]], axis=1).astype(jnp.bfloat16)


def set_ends(entries, stream_key, least, largest):
    place = [jax.random.randint(jax.random.fold_in(stream_key, axis), (), 0, length) for axis, length in enumerate(entries.shape)]
    main_axis = entries.shape.index(max(entries.shape))
    next_to = place[:main_axis] + [(place[main_axis] + 1) % entries.shape[main_axis]] + place[main_axis + 1:]
    return entries.at[tuple(place)].set(least).at[tuple(next_to)].set(largest)


def block_scale(rng, extent, cuts, least, largest):
    loudness, own = 1.0, jax.random.fold_in(rng, 6)
    for axis_at, shards_of in cuts:
        steps = jnp.exp(jax.random.uniform(jax.random.fold_in(own, axis_at), (shards_of,), jnp.float32, least / len(cuts), largest / len(cuts)))
        loudness = loudness * jnp.repeat(steps, extent[axis_at] // shards_of).reshape([-1 if axis == axis_at else 1 for axis in range(len(extent))])
    return loudness


def noise(own_key, dims, scale, most, cuts=(), kind=jnp.bfloat16):
    values = scale * jax.random.normal(own_key, dims, jnp.float32)
    if cuts:
        values = values * block_scale(own_key, dims, cuts, -0.22, 0.18)
    return jnp.clip(values, -most, most).astype(kind)


def setup_inputs(seed: int = 0) -> dict:
    streams_of = jax.random.split(jax.random.key(seed), 10)
    return {
        "temporal": noise(streams_of[0], (FRAMES, D), 1.0, 6.0, ((0, 8), (1, 4))),
        "frame_ids": set_ends(jax.random.randint(streams_of[1], (FRAMES, CODEBOOKS), 0, CARD), jax.random.fold_in(streams_of[1], 1), 0, CARD - 1).astype(jnp.int32),
        "proj_weight": noise(streams_of[2], (CODEBOOKS, D, DD), D ** -0.5, 0.09375, ((0, 4), (1, 4))),
        "embed_table": noise(streams_of[3], (CODEBOOKS, CARD + 1, DD), 1.0, 6.0, ((0, 4),)),
        "qkv_weight": draw_qkv_weight(jax.random.fold_in(streams_of[9], 71), 0),
        "out_weight": noise(streams_of[5], (CODEBOOKS, DD, DD), DD ** -0.5, 0.1875, ((0, 4), (1, 4))),
        "gate_up": noise(streams_of[6], (CODEBOOKS, 2, DD, HID), DD ** -0.5, 0.1875, ((0, 4), (3, 4))),
        "down_weight": noise(streams_of[7], (CODEBOOKS, HID, DD), HID ** -0.5, 0.09375, ((0, 4), (1, 4))),
        "norm_gains": jnp.clip(1.0 + 0.15 * jax.random.normal(streams_of[8], (CODEBOOKS, 2, DD), jnp.float32), 0.25, 1.75),
    }


def normalize(values, gain):
    return values * lax.rsqrt(lax.optimization_barrier(jnp.mean(values * values, axis=-1, keepdims=True)) + 1e-05) * gain

def attend(queries, keys, values):
    positions = queries.shape[0]
    head_size = queries.shape[-1]
    scores = jnp.einsum('ifhd,jfhd->fhij', queries.astype(jnp.float32), keys.astype(jnp.float32)) * head_size ** (-0.5)
    causal = jnp.arange(positions)[:, None] >= jnp.arange(positions)[None, :]
    scores = jnp.where(causal, scores, -1e+30)
    highest = lax.optimization_barrier(jnp.max(scores, axis=-1, keepdims=True))
    weights = jnp.where(causal, jnp.exp(scores - highest), 0.0)
    running = lax.optimization_barrier(jnp.sum(weights, axis=-1))
    attended = jnp.einsum('fhij,jfhd->ifhd', weights.astype(jnp.bfloat16).astype(jnp.float32), values.astype(jnp.float32))
    return (attended / jnp.transpose(running, (2, 0, 1))[..., None]).astype(jnp.bfloat16)

def reference(temporal, frame_ids, proj_weight, embed_table, qkv_weight, out_weight, gate_up, down_weight, norm_gains):
    start_column = jnp.full((FRAMES, 1), CARD, jnp.int32)
    previous = jnp.concatenate([start_column, frame_ids[:, :-1].astype(jnp.int32)], axis=1)

    def first_half(inputs):
        projection, token_table, triple, norm_gain, token_ids = inputs
        x_zero = jnp.dot(temporal, projection, preferred_element_type=jnp.float32) + token_table[token_ids].astype(jnp.float32)
        normed = normalize(x_zero, norm_gain[0]).astype(jnp.bfloat16)
        outputs = [jnp.dot(normed, triple[i], preferred_element_type=jnp.float32).astype(jnp.bfloat16) for i in range(3)]
        return (x_zero, outputs[0], outputs[1], outputs[2])
    x_zero, queries, keys, values = lax.map(first_half, (proj_weight, embed_table, qkv_weight, norm_gains, previous.T))
    head_shape = (CODEBOOKS, FRAMES, HEADS, DD // HEADS)
    attended = attend(queries.reshape(head_shape), keys.reshape(head_shape), values.reshape(head_shape)).reshape(CODEBOOKS, FRAMES, DD)

    def second_half(inputs):
        base, attention, out_matrix, gate_pair, down_matrix, norm_gain = inputs
        residual = base + jnp.dot(attention, out_matrix, preferred_element_type=jnp.float32)
        normed = normalize(residual, norm_gain[1]).astype(jnp.bfloat16)
        gate_sum = jnp.dot(normed, gate_pair[0], preferred_element_type=jnp.float32)
        upper_sum = jnp.dot(normed, gate_pair[1], preferred_element_type=jnp.float32)
        activated = (jax.nn.silu(gate_sum) * upper_sum).astype(jnp.bfloat16)
        return residual + jnp.dot(activated, down_matrix, preferred_element_type=jnp.float32)
    return lax.map(second_half, (x_zero, attended, out_weight, gate_up, down_weight, norm_gains))
```

```python
import functools

import jax
import jax.numpy as jnp
from jax import lax
from jax.experimental import pallas as pl
from jax.experimental.pallas import tpu as pltpu
from jax.sharding import PartitionSpec as P

HEADS = 16
CHUNKS = 2
ROW_BLOCK = 128
F32 = jnp.float32
BF16 = jnp.bfloat16


def swap(block, axis, distance):
    count = lax.axis_size(axis)
    return lax.ppermute(block, axis, [(i, i ^ distance) for i in range(count)])


def bits_of(axis):
    count = lax.axis_size(axis)
    return [1 << b for b in range(count.bit_length() - 1)]


def shifted(block, axis, distance):
    devices = range(lax.axis_size(axis))
    route = [(i - distance, i) for i in devices if i - distance in devices]
    return lax.ppermute(block, axis, route)


def gathered(block, axis):
    pieces = block[None]
    index = lax.axis_index(axis)
    for bit in reversed(bits_of(axis)):
        other = swap(pieces, axis, bit)
        upper = (index & bit) != 0
        first = jnp.where(upper, other, pieces)
        second = jnp.where(upper, pieces, other)
        pieces = jnp.stack([first, second], axis=1).reshape((-1,) + block.shape)
    return pieces


def normalize(values, norm_gain):
    return values * lax.rsqrt(jnp.mean(values * values, axis=-1, keepdims=True) + 1e-05) * norm_gain


def dot(a, b):
    return jnp.dot(a, b, preferred_element_type=F32)


def attend_kernel(slots, head_size, code_ref, query_ref, *refs):
    kv_refs = refs[: len(slots)]
    weight_refs = refs[len(slots) : -2]
    part_ref, sent_ref = refs[-2:]
    code = code_ref[0]
    width = query_ref.shape[-1]
    lanes = 128
    column = lax.broadcasted_iota(jnp.int32, (width, lanes), 0) // head_size
    head = lax.broadcasted_iota(jnp.int32, (width, lanes), 1)
    gather = (column == head).astype(F32).astype(BF16)
    head_t = lax.broadcasted_iota(jnp.int32, (lanes, width), 0)
    column_t = lax.broadcasted_iota(jnp.int32, (lanes, width), 1) // head_size
    spread = (column_t == head_t).astype(F32).astype(BF16)
    query = query_ref[...].astype(F32)
    scores = []
    for slot, kv_ref in zip(slots, kv_refs):
        product = query * kv_ref[0].astype(F32)
        high = product.astype(BF16)
        low = (product - high.astype(F32)).astype(BF16)
        score = (dot(high, gather) + dot(low, gather)) * head_size ** (-0.5)
        if slot:
            score = jnp.where((code ^ slot) <= code, score, -1e30)
        scores.append(score)
    highest = functools.reduce(jnp.maximum, scores)
    weights = [jnp.exp(score - highest) for score in scores]
    running = functools.reduce(jnp.add, weights)
    summed = None
    for kv_ref, weight in zip(kv_refs, weights):
        term = dot(weight.astype(BF16), spread) * kv_ref[1].astype(F32)
        summed = term if summed is None else summed + term
    inverse = 1.0 / running
    high = inverse.astype(BF16)
    low = (inverse - high.astype(F32)).astype(BF16)
    attended = (summed * (dot(high, spread) + dot(low, spread))).astype(BF16)
    part, start = None, 0
    for weight_ref in weight_refs:
        depth = weight_ref.shape[0]
        term = dot(attended[:, start : start + depth], weight_ref[...])
        part = term if part is None else part + term
        start += depth
    part_ref[...] = part
    sent_ref[...] = part.astype(BF16)


def attend(code_index, query, slots, kvs, weights, head_size):
    rows, width = query.shape
    block = min(rows, ROW_BLOCK)
    out_width = weights[0].shape[1]
    row_spec = pl.BlockSpec((block, width), lambda r: (r, 0))
    kv_spec = pl.BlockSpec((2, block, width), lambda r: (0, r, 0))
    out_spec = pl.BlockSpec((block, out_width), lambda r: (r, 0))
    return pl.pallas_call(
        functools.partial(attend_kernel, slots, head_size),
        grid=(rows // block,),
        in_specs=[pl.BlockSpec(memory_space=pltpu.SMEM), row_spec]
        + [kv_spec] * len(kvs)
        + [pl.BlockSpec(w.shape, lambda r: (0, 0)) for w in weights],
        out_specs=[out_spec, out_spec],
        out_shape=[
            jax.ShapeDtypeStruct((rows, out_width), F32),
            jax.ShapeDtypeStruct((rows, out_width), BF16),
        ],
        compiler_params=pltpu.CompilerParams(vmem_limit_bytes=24 * 1024 * 1024),
        name="attend",
    )(code_index.reshape(1).astype(jnp.int32), query, *kvs, *weights)


def body(
    temporal,
    frame_ids,
    proj_weight,
    embed_table,
    qkv_weight,
    out_weight,
    gate_up,
    down_weight,
    norm_gains,
):
    code_index = lax.axis_index("codebook")
    hidden_index = lax.axis_index("hidden")
    frame_index = lax.axis_index("frames")
    hidden_bits = bits_of("hidden")
    pair_bit, far_bits = hidden_bits[0], hidden_bits[1:]
    odd = (hidden_index & pair_bit) != 0
    start_id = embed_table.shape[1] - 1
    norm_gain = norm_gains[0]
    width = embed_table.shape[2]
    local_width = qkv_weight.shape[3]
    head_size = width // HEADS

    pieces = gathered(temporal, "codebook")
    row_count = pieces.shape[0] * pieces.shape[1]
    half = row_count // 2
    step = half // CHUNKS
    halves = pieces.reshape(2, CHUNKS, step, pieces.shape[2])
    kept_rows = jnp.where(odd, halves[1], halves[0])
    sent_rows = jnp.where(odd, halves[0], halves[1])

    share = local_width // lax.axis_size("frames")
    qkv_share = lax.dynamic_slice_in_dim(qkv_weight[0], frame_index * share, share, 2)
    out_share = lax.dynamic_slice_in_dim(out_weight[0], frame_index * share, share, 0)
    qkv_shares = [swap(qkv_share, "hidden", pair_bit)]
    out_shares = [swap(out_share, "hidden", pair_bit)]
    for bit in bits_of("frames"):
        qkv_shares += [swap(piece, "frames", bit) for piece in qkv_shares]
        out_shares += [swap(piece, "frames", bit) for piece in out_shares]
    qkv_pieces = [qkv_weight[0]] + qkv_shares
    out_pieces = [out_weight[0]] + out_shares

    earlier = shifted(frame_ids, "codebook", 1)[:, 0]
    previous = jnp.where(code_index == 0, start_id, earlier).reshape(2, half)
    previous = jnp.where(odd, previous[1], previous[0])
    embedded = embed_table[0][previous].reshape(CHUNKS, step, width)

    order = hidden_index ^ jnp.array([i & ~pair_bit for i in range(lax.axis_size("hidden")) if not i & pair_bit])
    down_blocks = jnp.moveaxis(down_weight[0].reshape(-1, lax.axis_size("hidden"), local_width), 1, 0)
    down_kept = [lax.dynamic_index_in_dim(down_blocks, o, 0, False) for o in order]
    down_sent = [lax.dynamic_index_in_dim(down_blocks, o ^ pair_bit, 0, False) for o in order]

    results = []
    for c in range(CHUNKS):
        sent = dot(sent_rows[c], proj_weight[0]).astype(BF16)
        arrived = swap(sent, "hidden", pair_bit)
        total = dot(kept_rows[c], proj_weight[0]) + arrived.astype(F32)
        for bit in far_bits:
            total = total + swap(total.astype(BF16), "hidden", bit).astype(F32)
        x_zero = total + embedded[c].astype(F32)
        normed = normalize(x_zero, norm_gain[0]).astype(BF16)
        triples = [
            jnp.einsum("rd,kdc->krc", normed, piece, preferred_element_type=F32).astype(BF16)
            for piece in qkv_pieces
        ]
        triple = jnp.concatenate(triples, axis=2)
        query, kv = triple[0], triple[1:]
        kvs = {0: kv}
        for bit in reversed(bits_of("codebook")):
            kvs.update({slot ^ bit: swap(block, "codebook", bit) for slot, block in kvs.items()})
        slots = tuple(kvs)
        part, part_sent = attend(
            code_index, query, slots, [kvs[s] for s in slots], out_pieces, head_size
        )
        total = part
        part_sent = part_sent
        for i, bit in enumerate(far_bits):
            total = total + swap(part_sent if i == 0 else total.astype(BF16), "hidden", bit).astype(F32)
        residual = x_zero + total
        other = swap(residual.astype(BF16), "hidden", pair_bit).astype(F32)
        sums_kept, sums_sent = [], []
        for rows in (residual, other):
            normed_two = normalize(rows, norm_gain[1]).astype(BF16)
            gate_sum = dot(normed_two, gate_up[0, 0])
            upper_sum = dot(normed_two, gate_up[0, 1])
            activated = (jax.nn.silu(gate_sum) * upper_sum).astype(BF16)
            sums_sent.append(jnp.stack([dot(activated, w) for w in down_sent]).astype(BF16))
            sums_kept.append(jnp.stack([dot(activated, w) for w in down_kept]))
        arrived = swap(jnp.stack(sums_sent), "hidden", pair_bit).astype(F32)
        sums = jnp.stack(sums_kept) + arrived[::-1]
        blocks = sums.shape[1]
        for bit in far_bits[::-1]:
            blocks //= 2
            sums = sums[:, :blocks] + swap(sums[:, blocks:].astype(BF16), "hidden", bit).astype(F32)
        sums = sums[:, 0]
        start = hidden_index * local_width
        own = lax.dynamic_slice_in_dim(residual, start, local_width, 1) + sums[0]
        far = lax.dynamic_slice_in_dim(other, start, local_width, 1) + sums[1]
        results.append(jnp.stack([jnp.where(odd, far, own), jnp.where(odd, own, far)]))
    return jnp.stack(results, axis=1).reshape(1, row_count, local_width)


def solution(mesh):
    placed = (
        P(("frames", "codebook"), "hidden"),
        P("frames", "codebook"),
        P("codebook", "hidden", None),
        P("codebook", None, None),
        P("codebook", None, None, "hidden"),
        P("codebook", "hidden", None),
        P("codebook", None, None, "hidden"),
        P("codebook", "hidden", None),
        P("codebook", None, None),
    )
    return jax.shard_map(
        body,
        mesh=mesh,
        in_specs=placed,
        out_specs=P("codebook", "frames", "hidden"),
        check_vma=False,
    )
```

```python
import functools

import jax
import jax.numpy as jnp
from jax import lax
from jax.experimental import pallas as pl
from jax.experimental.pallas import tpu as pltpu
from jax.sharding import PartitionSpec as P

HEADS = 16
CHUNKS = 2
F32 = jnp.float32
BF16 = jnp.bfloat16


def swap(block, axis, distance):
    count = lax.axis_size(axis)
    return lax.ppermute(block, axis, [(i, i ^ distance) for i in range(count)])


def bits_of(axis):
    count = lax.axis_size(axis)
    return [1 << b for b in range(count.bit_length() - 1)]


def shifted(block, axis, distance):
    devices = range(lax.axis_size(axis))
    route = [(i - distance, i) for i in devices if i - distance in devices]
    return lax.ppermute(block, axis, route)


def slots_of(block, axis):
    slots = {0: block}
    for bit in reversed(bits_of(axis)):
        slots.update({slot ^ bit: swap(piece, axis, bit) for slot, piece in slots.items()})
    return slots


def dot(a, b):
    return jnp.dot(a, b, preferred_element_type=F32)


def normalize(values, norm_gain):
    return values * lax.rsqrt(jnp.mean(values * values, axis=-1, keepdims=True) + 1e-05) * norm_gain


def call(kernel, name, outs, args, scratch=()):
    return pl.pallas_call(
        kernel,
        name=name,
        out_shape=[jax.ShapeDtypeStruct(shape, dtype) for shape, dtype in outs],
        in_specs=[pl.BlockSpec(memory_space=pltpu.VMEM)] * len(args),
        out_specs=[pl.BlockSpec(memory_space=pltpu.VMEM)] * len(outs),
        scratch_shapes=list(scratch),
        cost_estimate=pl.CostEstimate(flops=1000, bytes_accessed=1000, transcendentals=0),
        compiler_params=pltpu.CompilerParams(vmem_limit_bytes=48 * 1024 * 1024),
    )(*args)


def row_blocks(rows):
    size = min(rows, 128)
    return [pl.ds(start, size) for start in range(0, rows, size)]


def proj_kernel(slots, chunk, flip, *refs):
    piece_refs, weight_ref, out_ref, rows_ref = refs[: len(slots)], *refs[len(slots) :]
    code = lax.axis_index("codebook")
    half = (lax.axis_index("hidden") & 1) ^ flip
    count = len(slots)
    each = count // 2 // CHUNKS
    size = piece_refs[0].shape[0]
    for i in range(each):
        wanted = code ^ (half * (count // 2) + chunk * each + i)
        for slot, piece_ref in zip(slots, piece_refs):

            @pl.when(wanted == slot)
            def _():
                rows_ref[...] = piece_ref[...]

        out_ref[pl.ds(i * size, size), :] = dot(rows_ref[...], weight_ref[0]).astype(out_ref.dtype)


def embed_kernel(chunk, ids_ref, table_ref, out_ref):
    half = lax.axis_index("hidden") & 1
    first = lax.axis_index("codebook") == 0
    rows = out_ref.shape[0]
    start_id = table_ref.shape[0] - 1
    for block in row_blocks(rows):
        offset = half * (ids_ref.shape[0] // 2) + chunk * rows + block.start
        ids = ids_ref[pl.ds(pl.multiple_of(offset, 8), block.size), :]
        ids = jnp.where(first, start_id, ids)
        token = lax.broadcasted_iota(jnp.int32, (block.size, start_id), 1)
        chosen = (token == ids).astype(F32).astype(BF16)
        started = jnp.where(ids == start_id, 1.0, 0.0) * table_ref[start_id:, :].astype(F32)
        out_ref[block, :] = (dot(chosen, table_ref[:start_id, :]) + started).astype(BF16)


def qkv_kernel(rows_ref, gain_ref, weight_ref, query_ref, kv_ref):
    for block in row_blocks(rows_ref.shape[0]):
        normed = normalize(rows_ref[block, :].astype(F32), gain_ref[0, 0:1, :]).astype(BF16)
        query_ref[block, :] = dot(normed, weight_ref[0, 0]).astype(BF16)
        kv_ref[0, block, :] = dot(normed, weight_ref[0, 1]).astype(BF16)
        kv_ref[1, block, :] = dot(normed, weight_ref[0, 2]).astype(BF16)


def attend_kernel(slots, head_size, query_ref, *refs):
    kv_refs = refs[: len(slots)]
    weight_ref, part_ref = refs[len(slots) :]
    code = lax.axis_index("codebook")
    width = query_ref.shape[-1]
    lanes = 128
    column = lax.broadcasted_iota(jnp.int32, (width, lanes), 0) // head_size
    head = lax.broadcasted_iota(jnp.int32, (width, lanes), 1)
    gather = (column == head).astype(F32).astype(BF16)
    head_t = lax.broadcasted_iota(jnp.int32, (lanes, width), 0)
    column_t = lax.broadcasted_iota(jnp.int32, (lanes, width), 1) // head_size
    spread = (column_t == head_t).astype(F32).astype(BF16)
    for block in row_blocks(query_ref.shape[0]):
        query = query_ref[block, :].astype(F32)
        scores = []
        for slot, kv_ref in zip(slots, kv_refs):
            product = query * kv_ref[0, block, :].astype(F32)
            high = product.astype(BF16)
            low = (product - high.astype(F32)).astype(BF16)
            score = (dot(high, gather) + dot(low, gather)) * head_size ** (-0.5)
            if slot:
                score = jnp.where((code ^ slot) <= code, score, -1e30)
            scores.append(score)
        highest = functools.reduce(jnp.maximum, scores)
        weights = [jnp.exp(score - highest) for score in scores]
        running = functools.reduce(jnp.add, weights)
        summed = None
        for kv_ref, weight in zip(kv_refs, weights):
            term = dot(weight.astype(BF16), spread) * kv_ref[1, block, :].astype(F32)
            summed = term if summed is None else summed + term
        inverse = 1.0 / running
        high = inverse.astype(BF16)
        low = (inverse - high.astype(F32)).astype(BF16)
        attended = (summed * (dot(high, spread) + dot(low, spread))).astype(BF16)
        part_ref[block, :] = dot(attended, weight_ref[0]).astype(part_ref.dtype)


def mlp_kernel(count, rows_ref, gain_ref, gate_up_ref, down_ref, kept_ref, sent_ref, act_ref):
    index = lax.axis_index("hidden")
    hidden = act_ref.shape[1]
    step = min(hidden, 256)
    width = kept_ref.shape[2]
    for block in row_blocks(rows_ref.shape[0]):
        normed = normalize(rows_ref[block, :].astype(F32), gain_ref[0, 1:2, :]).astype(BF16)
        for start in range(0, hidden, step):
            columns = pl.ds(start, step)
            gate_sum = dot(normed, gate_up_ref[0, 0, :, columns])
            upper_sum = dot(normed, gate_up_ref[0, 1, :, columns])
            act_ref[:, columns] = (jax.nn.silu(gate_sum) * upper_sum).astype(BF16)
        for i in range(count // 2):
            owner = index ^ (2 * i)
            columns = pl.ds(pl.multiple_of((owner ^ 1) * width, width), width)
            sent_ref[i, block, :] = dot(act_ref[...], down_ref[0, :, columns]).astype(BF16)
        for i in range(count // 2):
            owner = index ^ (2 * i)
            columns = pl.ds(pl.multiple_of(owner * width, width), width)
            total = dot(act_ref[...], down_ref[0, :, columns])
            if i == 0:
                total = total + rows_ref[block, columns].astype(F32)
            kept_ref[i, block, :] = total


def body(
    temporal,
    frame_ids,
    proj_weight,
    embed_table,
    qkv_weight,
    out_weight,
    gate_up,
    down_weight,
    norm_gains,
):
    hidden_count = lax.axis_size("hidden")
    pair_bit, *far_bits = bits_of("hidden")
    odd = (lax.axis_index("hidden") & pair_bit) != 0
    width = embed_table.shape[2]
    local_width = qkv_weight.shape[3]
    head_size = width // HEADS
    table = embed_table[0]

    pieces = slots_of(temporal, "codebook")
    slots = tuple(pieces)
    pieces = [pieces[slot] for slot in slots]
    row_count = len(slots) * temporal.shape[0]
    rows = row_count // 2 // CHUNKS
    earlier = shifted(frame_ids, "codebook", 1)

    def project(c, flip, dtype):
        return call(
            functools.partial(proj_kernel, slots, c, flip),
            "project",
            [((rows, width), dtype)],
            [*pieces, proj_weight],
            [pltpu.VMEM(temporal.shape, BF16)],
        )[0]

    def qkv(block):
        return call(
            qkv_kernel,
            "qkv",
            [((rows, local_width), BF16), ((2, rows, local_width), BF16)],
            [block, norm_gains, qkv_weight],
        )

    def attend(query, kv, dtype):
        kvs = slots_of(kv, "codebook")
        order = tuple(sorted(kvs))
        return call(
            functools.partial(attend_kernel, order, head_size),
            "attend",
            [((rows, width), dtype)],
            [query, *[kvs[slot] for slot in order], out_weight],
        )[0]

    def mlp(block):
        shape = (hidden_count // 2, rows, local_width)
        return call(
            functools.partial(mlp_kernel, hidden_count),
            "mlp",
            [(shape, F32), (shape, BF16)],
            [block, norm_gains, gate_up, down_weight],
            [pltpu.VMEM((min(rows, 128), gate_up.shape[3]), BF16)],
        )

    results = []
    for c in range(CHUNKS):
        arrived = swap(project(c, 1, BF16), "hidden", pair_bit)
        total = project(c, 0, F32) + arrived.astype(F32)
        embedded = call(
            functools.partial(embed_kernel, c), "embed", [((rows, width), BF16)], [earlier, table]
        )[0]
        for bit in far_bits:
            total = total + swap(total.astype(BF16), "hidden", bit).astype(F32)
        x_zero = total + embedded.astype(F32)
        x_other = swap(x_zero.astype(BF16), "hidden", pair_bit)
        part_own = attend(*qkv(x_zero), F32)
        part_other = attend(*qkv(x_other), BF16)
        total = part_own + swap(part_other, "hidden", pair_bit).astype(F32)
        for bit in far_bits:
            total = total + swap(total.astype(BF16), "hidden", bit).astype(F32)
        residual = x_zero + total
        other = swap(residual.astype(BF16), "hidden", pair_bit)
        own_kept, own_sent = mlp(residual)
        other_kept, other_sent = mlp(other)
        arrived = swap(jnp.stack([other_sent, own_sent]), "hidden", pair_bit).astype(F32)
        sums = jnp.stack([own_kept, other_kept]) + arrived
        blocks = sums.shape[1]
        for bit in far_bits[::-1]:
            blocks //= 2
            sums = sums[:, :blocks] + swap(sums[:, blocks:].astype(BF16), "hidden", bit).astype(F32)
        own, far = sums[0, 0], sums[1, 0]
        results.append(jnp.stack([jnp.where(odd, far, own), jnp.where(odd, own, far)]))
    return jnp.stack(results, axis=1).reshape(1, row_count, local_width)


def solution(mesh):
    placed = (
        P(("frames", "codebook"), "hidden"),
        P("frames", "codebook"),
        P("codebook", "hidden", None),
        P("codebook", None, None),
        P("codebook", None, None, "hidden"),
        P("codebook", "hidden", None),
        P("codebook", None, None, "hidden"),
        P("codebook", "hidden", None),
        P("codebook", None, None),
    )
    return jax.shard_map(
        body,
        mesh=mesh,
        in_specs=placed,
        out_specs=P("codebook", "frames", "hidden"),
        check_vma=False,
    )
```

```python
import functools
import math

import jax
import jax.numpy as jnp
from jax import lax
from jax.experimental import pallas as pl
from jax.experimental.pallas import tpu as pltpu
from jax.sharding import PartitionSpec as P

HEADS = 16
CHUNKS = 4
SPLITS = 2
F32 = jnp.float32
BF16 = jnp.bfloat16
VMEM = pl.BlockSpec(memory_space=pltpu.VMEM)


def swap(block, axis, distance):
    count = lax.axis_size(axis)
    return lax.ppermute(block, axis, [(i, i ^ distance) for i in range(count)])


def middle_swap(block):
    ends, codes = lax.axis_size("hidden"), lax.axis_size("codebook")
    route = []
    for code in range(codes):
        for i in range(ends):
            other = (code, ends - 1 - i) if 0 < i < ends - 1 else (code ^ 1, i)
            route.append((code * ends + i, other[0] * ends + other[1]))
    return lax.ppermute(block, ("codebook", "hidden"), route)


def is_middle():
    index = lax.axis_index("hidden")
    return (index > 0) & (index < lax.axis_size("hidden") - 1)


def bits_of(axis):
    count = lax.axis_size(axis)
    return [1 << b for b in range(count.bit_length() - 1)]


def shifted(block, axis, distance):
    devices = range(lax.axis_size(axis))
    route = [(i - distance, i) for i in devices if i - distance in devices]
    return lax.ppermute(block, axis, route)


def slots_of(block, axis):
    slots = {0: block}
    for bit in reversed(bits_of(axis)):
        slots.update({slot ^ bit: swap(piece, axis, bit) for slot, piece in slots.items()})
    return [slots[slot] for slot in range(len(slots))]


def dot(a, b):
    return jnp.dot(a, b, preferred_element_type=F32)


def normalize(values, norm_gain):
    return values * lax.rsqrt(jnp.mean(values * values, axis=-1, keepdims=True) + 1e-05) * norm_gain


class Steps:
    def __init__(self):
        self.token = None

    def __call__(self, kernel, name, outs, args, scratch=(), aliases=None, out_space=pltpu.VMEM):
        tokens = [] if self.token is None else [self.token]
        count, given = len(outs), len(args)
        held = [(a.shape, a.dtype) for a in args] + list(outs)
        size = sum(math.prod(shape) * jnp.dtype(dtype).itemsize for shape, dtype in held)

        def with_token(*refs):
            inputs, rest = refs[:given], refs[given + len(tokens) :]
            outputs, token_ref, scratches = rest[:count], rest[count], rest[count + 1 :]
            kernel(*inputs, *outputs, *scratches)
            token_ref[...] = jnp.zeros_like(token_ref)

        *results, self.token = pl.pallas_call(
            with_token,
            name=name,
            out_shape=[jax.ShapeDtypeStruct(shape, dtype) for shape, dtype in outs]
            + [jax.ShapeDtypeStruct((8, 128), F32)],
            in_specs=[VMEM] * (given + len(tokens)),
            out_specs=[pl.BlockSpec(memory_space=out_space)] * count + [VMEM],
            scratch_shapes=list(scratch),
            input_output_aliases=aliases or {},
            cost_estimate=pl.CostEstimate(flops=1000, bytes_accessed=1000, transcendentals=0),
            compiler_params=pltpu.CompilerParams(vmem_limit_bytes=size + (6 << 20)),
        )(*args, *tokens)
        return results


def row_blocks(rows):
    size = min(rows, 128)
    return [pl.ds(start, size) for start in range(0, rows, size)]


def proj_kernel(start, *refs):
    *piece_refs, weight_ref, out_ref, rows_ref = refs
    code = lax.axis_index("codebook")
    size = rows_ref.shape[0] // len(piece_refs)
    for i in range(len(piece_refs)):
        for slot, piece_ref in enumerate(piece_refs):

            @pl.when(code ^ i == slot)
            def _():
                rows_ref[i * size : (i + 1) * size, :] = piece_ref[start : start + size, :]

    for block in row_blocks(rows_ref.shape[0]):
        out_ref[block, :] = dot(rows_ref[block, :], weight_ref[0])


def embed_kernel(chunk, ids_ref, table_ref, out_ref):
    first = lax.axis_index("codebook") == 0
    start_id = table_ref.shape[1] - 1
    count, length = ids_ref.shape
    size = out_ref.shape[0] // count
    diagonal = lax.broadcasted_iota(jnp.int32, (length, length), 0) == lax.broadcasted_iota(
        jnp.int32, (length, length), 1
    )
    columns = []
    for i in range(count):
        line = ids_ref[i : i + 1, :].astype(F32)
        column = jnp.sum(jnp.where(diagonal, line, 0.0), axis=1, keepdims=True).astype(jnp.int32)
        columns.append(column[chunk * size : (chunk + 1) * size])
    all_ids = jnp.where(first, start_id, jnp.concatenate(columns, axis=0))
    for block in row_blocks(out_ref.shape[0]):
        ids = all_ids[block.start : block.start + block.size]
        token = lax.broadcasted_iota(jnp.int32, (block.size, start_id), 1)
        chosen = (token == ids).astype(F32).astype(BF16)
        started = jnp.where(ids == start_id, 1.0, 0.0) * table_ref[0, start_id:, :].astype(F32)
        out_ref[block, :] = (dot(chosen, table_ref[0, :start_id, :]) + started).astype(BF16)


def sum_kernel(*refs):
    *term_refs, wide_ref, sent_ref = refs
    total = term_refs[0][...].astype(F32)
    for term_ref in term_refs[1:]:
        total = total + term_ref[...].astype(F32)
    wide_ref[...] = total
    sent_ref[...] = total.astype(BF16)


def pass_kernel(given_ref, taken_ref):
    pass


def mix_kernel(terms, *refs):
    outs = 2 if terms else 1
    sent_ref = refs[-1]
    part_refs, term_refs = refs[: len(refs) - outs - terms], refs[len(refs) - outs - terms : -outs]

    def send_part():
        sent_ref[...] = part_refs[0][...].astype(BF16)

    def send_rows():
        total = term_refs[0][...].astype(F32)
        for term_ref in term_refs[1:]:
            total = total + term_ref[...].astype(F32)
        refs[-2][...] = total
        sent_ref[...] = total.astype(BF16)

    if not term_refs:
        send_part()
    elif not part_refs:
        send_rows()
    else:
        pl.when(is_middle())(send_rows)
        pl.when(jnp.logical_not(is_middle()))(send_part)


def choose(wide_ref, arrived_ref, rows_ref):
    @pl.when(is_middle())
    def _():
        rows_ref[...] = wide_ref[...]

    @pl.when(jnp.logical_not(is_middle()))
    def _():
        rows_ref[...] = arrived_ref[...].astype(F32)


def qkv_kernel(wide_ref, arrived_ref, gain_ref, weight_ref, query_ref, kv_ref, rows_ref):
    choose(wide_ref, arrived_ref, rows_ref)
    for block in row_blocks(rows_ref.shape[0]):
        normed = normalize(rows_ref[block, :].astype(F32), gain_ref[0, 0:1, :]).astype(BF16)
        query_ref[block, :] = dot(normed, weight_ref[0, 0]).astype(BF16)
        kv_ref[0, block, :] = dot(normed, weight_ref[0, 1]).astype(BF16)
        kv_ref[1, block, :] = dot(normed, weight_ref[0, 2]).astype(BF16)


def attend_kernel(head_size, query_ref, *refs):
    *kv_refs, weight_ref, part_ref = refs
    code = lax.axis_index("codebook")
    width = query_ref.shape[-1]
    lanes = 128
    column = lax.broadcasted_iota(jnp.int32, (width, lanes), 0) // head_size
    head = lax.broadcasted_iota(jnp.int32, (width, lanes), 1)
    gather = (column == head).astype(F32).astype(BF16)
    head_t = lax.broadcasted_iota(jnp.int32, (lanes, width), 0)
    column_t = lax.broadcasted_iota(jnp.int32, (lanes, width), 1) // head_size
    spread = (column_t == head_t).astype(F32).astype(BF16)
    for block in row_blocks(query_ref.shape[0]):
        query = query_ref[block, :].astype(F32)
        scores = []
        for slot, kv_ref in enumerate(kv_refs):
            product = query * kv_ref[0, block, :].astype(F32)
            high = product.astype(BF16)
            low = (product - high.astype(F32)).astype(BF16)
            score = (dot(high, gather) + dot(low, gather)) * head_size ** (-0.5)
            if slot:
                score = jnp.where((code ^ slot) <= code, score, -1e30)
            scores.append(score)
        highest = functools.reduce(jnp.maximum, scores)
        weights = [jnp.exp(score - highest) for score in scores]
        running = functools.reduce(jnp.add, weights)
        summed = None
        for kv_ref, weight in zip(kv_refs, weights):
            term = dot(weight.astype(BF16), spread) * kv_ref[1, block, :].astype(F32)
            summed = term if summed is None else summed + term
        inverse = 1.0 / running
        high = inverse.astype(BF16)
        low = (inverse - high.astype(F32)).astype(BF16)
        attended = (summed * (dot(high, spread) + dot(low, spread))).astype(BF16)
        part_ref[block, :] = dot(attended, weight_ref[0]).astype(part_ref.dtype)


def mlp_kernel(
    count, wide_ref, arrived_ref, gain_ref, gate_up_ref, down_ref, kept_ref, sent_ref, rows_ref, act_ref
):
    choose(wide_ref, arrived_ref, rows_ref)
    index = lax.axis_index("hidden")
    hidden = act_ref.shape[1]
    step = min(hidden, 256)
    width = kept_ref.shape[2]
    for block in row_blocks(rows_ref.shape[0]):
        normed = normalize(rows_ref[block, :], gain_ref[0, 1:2, :]).astype(BF16)
        for start in range(0, hidden, step):
            columns = pl.ds(start, step)
            gate_sum = dot(normed, gate_up_ref[0, 0, :, columns])
            upper_sum = dot(normed, gate_up_ref[0, 1, :, columns])
            act_ref[:, columns] = (jax.nn.silu(gate_sum) * upper_sum).astype(BF16)
        for i in range(count // 2):
            owner = index ^ (2 * i)
            columns = pl.ds(pl.multiple_of((owner ^ 1) * width, width), width)
            sent_ref[i, block, :] = dot(act_ref[...], down_ref[0, :, columns]).astype(BF16)
        for i in range(count // 2):
            owner = index ^ (2 * i)
            columns = pl.ds(pl.multiple_of(owner * width, width), width)
            total = dot(act_ref[...], down_ref[0, :, columns])
            if i == 0:
                total = total + rows_ref[block, columns]
            kept_ref[i, block, :] = total


def halve_kernel(mine_ref, arrived_ref, wide_ref, sent_ref):
    kept = wide_ref.shape[0]
    wide_ref[...] = mine_ref[:kept] + arrived_ref[:kept].astype(F32)
    sent_ref[...] = (mine_ref[kept:] + arrived_ref[kept:].astype(F32)).astype(BF16)


def final_kernel(count, *refs):
    *in_refs, out_ref, rows_ref, sems = refs
    chunks = len(in_refs) // 2
    stride = out_ref.shape[1] // count
    size = stride // chunks
    copies = []
    for chunk in range(chunks):
        wide_ref, arrived_ref = in_refs[2 * chunk : 2 * chunk + 2]
        rows_ref[chunk] = wide_ref[0] + arrived_ref[0].astype(F32)
        for i in range(count):
            source = rows_ref.at[chunk, pl.ds(i * size, size), :]
            target = out_ref.at[0, pl.ds(i * stride + chunk * size, size), :]
            copies.append(pltpu.make_async_copy(source, target, sems.at[chunk, i]))
            copies[-1].start()
    for copy in copies:
        copy.wait()


def body(
    temporal,
    frame_ids,
    proj_weight,
    embed_table,
    qkv_weight,
    out_weight,
    gate_up,
    down_weight,
    norm_gains,
):
    hidden_count = lax.axis_size("hidden")
    code_count = lax.axis_size("codebook")
    pair_bit, far_bit = bits_of("hidden")
    code_bits = bits_of("codebook")[::-1]
    width = embed_table.shape[2]
    local_width = qkv_weight.shape[3]
    head_size = width // HEADS

    block_rows = temporal.shape[0]
    size = block_rows // CHUNKS
    rows = code_count * size
    row_count = code_count * block_rows
    split = block_rows // SPLITS
    pieces = [slots_of(temporal[i * split : (i + 1) * split], "codebook") for i in range(SPLITS)]
    earlier = shifted(frame_ids.reshape(code_count, -1), "codebook", 1)
    step = Steps()
    wide, sent = ((rows, width), F32), ((rows, width), BF16)
    states = [{} for _ in range(CHUNKS)]

    def get(c):
        return states[c] if 0 <= c < CHUNKS else None

    def project(c):
        if (s := get(c)) is not None:
            s["part"] = step(
                functools.partial(proj_kernel, c * size % split),
                "project",
                [wide],
                [*pieces[c * size // split], proj_weight],
                [pltpu.VMEM((rows, temporal.shape[1]), BF16)],
            )[0]

    def embed(c):
        if (s := get(c)) is not None:
            s["embedded"] = step(
                functools.partial(embed_kernel, c), "embed", [sent], [earlier, embed_table]
            )[0]

    def mix(c, older, part, terms, names):
        s, o = get(c), get(older)
        if s is None and o is None:
            return
        args = [s[part]] if s is not None else []
        given = [o[term] for term in terms] if o is not None else []
        outs = [wide, sent] if given else [sent]
        *finished, out = step(
            functools.partial(mix_kernel, len(given)), names[0], outs, [*args, *given]
        )
        arrived = swap(out, "hidden", pair_bit)
        if s is not None:
            s["arrived"] = arrived
        if o is not None:
            o[names[0]], o[names[1]] = finished[0], arrived

    def pair_sum(c):
        if (s := get(c)) is not None:
            s["total"], out = step(sum_kernel, "pair_sum", [wide, sent], [s["part"], s["arrived"]])
            s["far"] = middle_swap(out)

    def qkv(c):
        if (s := get(c)) is not None:
            s["query"], kv = step(
                qkv_kernel,
                "qkv",
                [((rows, local_width), BF16), ((2, rows, local_width), BF16)],
                [s["x_zero"], s["x_arrived"], norm_gains, qkv_weight],
                [pltpu.VMEM((rows, width), F32)],
            )
            s["kvs"] = {0: kv} | {bit: swap(kv, "codebook", bit) for bit in code_bits}

    def forward(c):
        if (s := get(c)) is not None:
            for bit in code_bits:
                for slot in [slot for slot in s["kvs"] if slot > bit and not slot & (2 * bit - 1)]:
                    (kv,) = step(pass_kernel, "pass", [((2, rows, local_width), BF16)], [s["kvs"][slot]], aliases={0: 0})
                    s["kvs"][slot ^ bit] = swap(kv, "codebook", bit)

    def attend(c):
        if (s := get(c)) is not None:
            s["part"] = step(
                functools.partial(attend_kernel, head_size),
                "attend",
                [wide],
                [s["query"], *[s["kvs"][slot] for slot in range(code_count)], out_weight],
            )[0]

    def mlp(c):
        if (s := get(c)) is not None:
            shape = (hidden_count // 2, rows, local_width)
            s["sums"], out = step(
                functools.partial(mlp_kernel, hidden_count),
                "mlp",
                [(shape, F32), (shape, BF16)],
                [s["residual"], s["residual_arrived"], norm_gains, gate_up, down_weight],
                [pltpu.VMEM((rows, width), F32), pltpu.VMEM((min(rows, 128), gate_up.shape[3]), BF16)],
            )
            s["sums_arrived"] = swap(out, "hidden", pair_bit)

    def halve(c):
        if (s := get(c)) is not None:
            shape = (hidden_count // 4, rows, local_width)
            s["wide"], out = step(
                halve_kernel, "halve", [(shape, F32), (shape, BF16)], [s["sums"], s["sums_arrived"]]
            )
            s["last"] = swap(out, "hidden", far_bit)

    def final():
        args = [s[name] for s in states for name in ("wide", "last")]
        return step(
            functools.partial(final_kernel, code_count),
            "final",
            [((1, row_count, local_width), F32)],
            args,
            [pltpu.VMEM((CHUNKS, rows, local_width), F32), pltpu.SemaphoreType.DMA((CHUNKS, code_count))],
            out_space=pl.ANY,
        )[0]

    stages = 9
    project(0)
    for t in range(CHUNKS + stages - 1):
        pair_sum(t - 1)
        mix(t, t - 2, "part", ["total", "far", "embedded"], ["x_zero", "x_arrived"])
        qkv(t - 3)
        attend(t - 4)
        mlp(t - 7)
        mix(t - 4, t - 6, "part", ["x_zero", "total", "far"], ["residual", "residual_arrived"])
        pair_sum(t - 5)
        halve(t - 8)
        project(t + 1)
        embed(t - 1)
        forward(t - 3)
    return final()


def solution(mesh):
    placed = (
        P(("frames", "codebook"), "hidden"),
        P("frames", "codebook"),
        P("codebook", "hidden", None),
        P("codebook", None, None),
        P("codebook", None, None, "hidden"),
        P("codebook", "hidden", None),
        P("codebook", None, None, "hidden"),
        P("codebook", "hidden", None),
        P("codebook", None, None),
    )
    return jax.shard_map(
        body,
        mesh=mesh,
        in_specs=placed,
        out_specs=P("codebook", "frames", "hidden"),
        check_vma=False,
    )
```

```python
import functools
import math

import jax
import jax.numpy as jnp
from jax import lax
from jax.experimental import pallas as pl
from jax.experimental.pallas import tpu as pltpu
from jax.sharding import PartitionSpec as P

HEADS = 16
CHUNKS = 4
SPLITS = 2
F32 = jnp.float32
BF16 = jnp.bfloat16
VMEM = pl.BlockSpec(memory_space=pltpu.VMEM)


def swap(block, axis, distance):
    count = lax.axis_size(axis)
    return lax.ppermute(block, axis, [(i, i ^ distance) for i in range(count)])


def middle_swap(block):
    ends, codes = lax.axis_size("hidden"), lax.axis_size("codebook")
    route = []
    for code in range(codes):
        for i in range(ends):
            other = (code, ends - 1 - i) if 0 < i < ends - 1 else (code ^ 1, i)
            route.append((code * ends + i, other[0] * ends + other[1]))
    return lax.ppermute(block, ("codebook", "hidden"), route)


def is_middle():
    index = lax.axis_index("hidden")
    return (index > 0) & (index < lax.axis_size("hidden") - 1)


def bits_of(axis):
    count = lax.axis_size(axis)
    return [1 << b for b in range(count.bit_length() - 1)]


def shifted(block, axis, distance):
    devices = range(lax.axis_size(axis))
    route = [(i - distance, i) for i in devices if i - distance in devices]
    return lax.ppermute(block, axis, route)


def slots_of(block, axis):
    slots = {0: block}
    for bit in reversed(bits_of(axis)):
        slots.update({slot ^ bit: swap(piece, axis, bit) for slot, piece in slots.items()})
    return [slots[slot] for slot in range(len(slots))]


def dot(a, b):
    return jnp.dot(a, b, preferred_element_type=F32)


def normalize(values, norm_gain):
    return values * lax.rsqrt(jnp.mean(values * values, axis=-1, keepdims=True) + 1e-05) * norm_gain


class Steps:
    def __init__(self):
        self.token = None

    def __call__(self, kernel, name, outs, args, scratch=(), aliases=None, out_space=pltpu.VMEM):
        tokens = [] if self.token is None else [self.token]
        count, given = len(outs), len(args)
        held = [(a.shape, a.dtype) for a in args] + list(outs)
        size = sum(math.prod(shape) * jnp.dtype(dtype).itemsize for shape, dtype in held)

        def with_token(*refs):
            inputs, rest = refs[:given], refs[given + len(tokens) :]
            outputs, token_ref, scratches = rest[:count], rest[count], rest[count + 1 :]
            kernel(*inputs, *outputs, *scratches)
            token_ref[...] = jnp.zeros_like(token_ref)

        *results, self.token = pl.pallas_call(
            with_token,
            name=name,
            out_shape=[jax.ShapeDtypeStruct(shape, dtype) for shape, dtype in outs]
            + [jax.ShapeDtypeStruct((8, 128), F32)],
            in_specs=[VMEM] * (given + len(tokens)),
            out_specs=[pl.BlockSpec(memory_space=out_space)] * count + [VMEM],
            scratch_shapes=list(scratch),
            input_output_aliases=aliases or {},
            cost_estimate=pl.CostEstimate(flops=1000, bytes_accessed=1000, transcendentals=0),
            compiler_params=pltpu.CompilerParams(vmem_limit_bytes=size + (6 << 20)),
        )(*args, *tokens)
        return results


def row_blocks(rows):
    size = min(rows, 128)
    return [pl.ds(start, size) for start in range(0, rows, size)]


def proj_kernel(start, *refs):
    *piece_refs, weight_ref, out_ref, rows_ref = refs
    code = lax.axis_index("codebook")
    size = rows_ref.shape[0] // len(piece_refs)
    for i in range(len(piece_refs)):
        for slot, piece_ref in enumerate(piece_refs):

            @pl.when(code ^ i == slot)
            def _():
                rows_ref[i * size : (i + 1) * size, :] = piece_ref[start : start + size, :]

    for block in row_blocks(rows_ref.shape[0]):
        out_ref[block, :] = dot(rows_ref[block, :], weight_ref[0])


def embed_kernel(chunk, ids_ref, table_ref, out_ref):
    first = lax.axis_index("codebook") == 0
    start_id = table_ref.shape[1] - 1
    count, length = ids_ref.shape
    size = out_ref.shape[0] // count
    diagonal = lax.broadcasted_iota(jnp.int32, (length, length), 0) == lax.broadcasted_iota(
        jnp.int32, (length, length), 1
    )
    columns = []
    for i in range(count):
        line = ids_ref[i : i + 1, :].astype(F32)
        column = jnp.sum(jnp.where(diagonal, line, 0.0), axis=1, keepdims=True).astype(jnp.int32)
        columns.append(column[chunk * size : (chunk + 1) * size])
    all_ids = jnp.where(first, start_id, jnp.concatenate(columns, axis=0))
    for block in row_blocks(out_ref.shape[0]):
        ids = all_ids[block.start : block.start + block.size]
        token = lax.broadcasted_iota(jnp.int32, (block.size, start_id), 1)
        chosen = (token == ids).astype(F32).astype(BF16)
        started = jnp.where(ids == start_id, 1.0, 0.0) * table_ref[0, start_id:, :].astype(F32)
        out_ref[block, :] = (dot(chosen, table_ref[0, :start_id, :]) + started).astype(BF16)


def sum_kernel(*refs):
    *term_refs, wide_ref, sent_ref = refs
    total = term_refs[0][...].astype(F32)
    for term_ref in term_refs[1:]:
        total = total + term_ref[...].astype(F32)
    wide_ref[...] = total
    sent_ref[...] = total.astype(BF16)


def pass_kernel(given_ref, taken_ref):
    pass


def mix_kernel(terms, *refs):
    outs = 2 if terms else 1
    sent_ref = refs[-1]
    part_refs, term_refs = refs[: len(refs) - outs - terms], refs[len(refs) - outs - terms : -outs]

    def send_part():
        sent_ref[...] = part_refs[0][...].astype(BF16)

    def send_rows():
        total = term_refs[0][...].astype(F32)
        for term_ref in term_refs[1:]:
            total = total + term_ref[...].astype(F32)
        refs[-2][...] = total
        sent_ref[...] = total.astype(BF16)

    if not term_refs:
        send_part()
    elif not part_refs:
        send_rows()
    else:
        pl.when(is_middle())(send_rows)
        pl.when(jnp.logical_not(is_middle()))(send_part)


def choose(wide_ref, arrived_ref, rows_ref):
    @pl.when(is_middle())
    def _():
        rows_ref[...] = wide_ref[...]

    @pl.when(jnp.logical_not(is_middle()))
    def _():
        rows_ref[...] = arrived_ref[...].astype(F32)


def qkv_kernel(wide_ref, arrived_ref, gain_ref, weight_ref, query_ref, kv_ref, rows_ref):
    choose(wide_ref, arrived_ref, rows_ref)
    for block in row_blocks(rows_ref.shape[0]):
        normed = normalize(rows_ref[block, :].astype(F32), gain_ref[0, 0:1, :]).astype(BF16)
        query_ref[block, :] = dot(normed, weight_ref[0, 0]).astype(BF16)
        kv_ref[0, block, :] = dot(normed, weight_ref[0, 1]).astype(BF16)
        kv_ref[1, block, :] = dot(normed, weight_ref[0, 2]).astype(BF16)


def attend_kernel(head_size, query_ref, *refs):
    *kv_refs, weight_ref, part_ref = refs
    code = lax.axis_index("codebook")
    width = query_ref.shape[-1]
    lanes = 128
    column = lax.broadcasted_iota(jnp.int32, (width, lanes), 0) // head_size
    head = lax.broadcasted_iota(jnp.int32, (width, lanes), 1)
    gather = (column == head).astype(F32).astype(BF16)
    head_t = lax.broadcasted_iota(jnp.int32, (lanes, width), 0)
    column_t = lax.broadcasted_iota(jnp.int32, (lanes, width), 1) // head_size
    spread = (column_t == head_t).astype(F32).astype(BF16)
    for block in row_blocks(query_ref.shape[0]):
        query = query_ref[block, :].astype(F32)
        scores = []
        for slot, kv_ref in enumerate(kv_refs):
            product = query * kv_ref[0, block, :].astype(F32)
            high = product.astype(BF16)
            low = (product - high.astype(F32)).astype(BF16)
            score = (dot(high, gather) + dot(low, gather)) * head_size ** (-0.5)
            if slot:
                score = jnp.where((code ^ slot) <= code, score, -1e30)
            scores.append(score)
        highest = functools.reduce(jnp.maximum, scores)
        weights = [jnp.exp(score - highest) for score in scores]
        running = functools.reduce(jnp.add, weights)
        summed = None
        for kv_ref, weight in zip(kv_refs, weights):
            term = dot(weight.astype(BF16), spread) * kv_ref[1, block, :].astype(F32)
            summed = term if summed is None else summed + term
        inverse = 1.0 / running
        high = inverse.astype(BF16)
        low = (inverse - high.astype(F32)).astype(BF16)
        attended = (summed * (dot(high, spread) + dot(low, spread))).astype(BF16)
        part_ref[block, :] = dot(attended, weight_ref[0]).astype(part_ref.dtype)


def mlp_kernel(count, whole, wide_ref, arrived_ref, gain_ref, gate_up_ref, down_ref, *refs):
    kept_ref, sent_ref, rows_ref, act_ref = refs
    choose(wide_ref, arrived_ref, rows_ref)
    index = lax.axis_index("hidden")
    hidden = act_ref.shape[1]
    step = min(hidden, 256)
    width = down_ref.shape[2] // count
    own = pl.ds(pl.multiple_of(index * width, width), width)
    for block in row_blocks(rows_ref.shape[0]):
        normed = normalize(rows_ref[block, :], gain_ref[0, 1:2, :]).astype(BF16)
        for start in range(0, hidden, step):
            columns = pl.ds(start, step)
            gate_sum = dot(normed, gate_up_ref[0, 0, :, columns])
            upper_sum = dot(normed, gate_up_ref[0, 1, :, columns])
            act_ref[:, columns] = (jax.nn.silu(gate_sum) * upper_sum).astype(BF16)
        if whole:
            total = dot(act_ref[...], down_ref[0])
            sent_ref[block, :] = total.astype(BF16)
            kept_ref[block, :] = total
            kept_ref[block, own] = kept_ref[block, own] + rows_ref[block, own]
            continue
        for i in range(count // 2):
            owner = index ^ (2 * i)
            columns = pl.ds(pl.multiple_of((owner ^ 1) * width, width), width)
            sent_ref[i, block, :] = dot(act_ref[...], down_ref[0, :, columns]).astype(BF16)
        for i in range(count // 2):
            owner = index ^ (2 * i)
            columns = pl.ds(pl.multiple_of(owner * width, width), width)
            total = dot(act_ref[...], down_ref[0, :, columns])
            if i == 0:
                total = total + rows_ref[block, columns]
            kept_ref[i, block, :] = total


def gather_kernel(mine_ref, arrived_ref, wide_ref, sent_ref):
    index = lax.axis_index("hidden")
    width = wide_ref.shape[2]
    far = lax.axis_size("hidden") - 1 - index

    def columns(owner):
        return pl.ds(pl.multiple_of(owner * width, width), width)

    def total(owner):
        return mine_ref[:, columns(owner)] + arrived_ref[:, columns(owner)].astype(F32)

    wide_ref[0] = total(index)
    wide_ref[1] = mine_ref[:, columns(index ^ 1)]
    sent_ref[0] = total(far).astype(BF16)
    sent_ref[1] = total(far ^ 1).astype(BF16)


def return_kernel(wide_ref, arrived_ref, own_ref, sent_ref):
    own_ref[...] = wide_ref[0] + arrived_ref[0].astype(F32)
    sent_ref[...] = (wide_ref[1] + arrived_ref[1].astype(F32)).astype(BF16)


def halve_kernel(mine_ref, arrived_ref, wide_ref, sent_ref):
    kept = wide_ref.shape[0]
    wide_ref[...] = mine_ref[:kept] + arrived_ref[:kept].astype(F32)
    sent_ref[...] = (mine_ref[kept:] + arrived_ref[kept:].astype(F32)).astype(BF16)


def final_kernel(count, routes, *refs):
    *in_refs, out_ref, rows_ref, sems = refs
    chunks = rows_ref.shape[0]
    stride = out_ref.shape[1] // count
    size = stride // chunks
    width = out_ref.shape[2]
    index = lax.axis_index("hidden")
    copies = []
    for chunk in range(chunks):
        if routes[chunk]:
            own_ref, mine_ref, arrived_ref, *in_refs = in_refs

            @pl.when(is_middle())
            def _():
                rows_ref[chunk] = own_ref[...]

            @pl.when(jnp.logical_not(is_middle()))
            def _():
                mine = mine_ref[:, pl.ds(pl.multiple_of(index * width, width), width)]
                rows_ref[chunk] = mine + arrived_ref[...].astype(F32)

        else:
            wide_ref, arrived_ref, *in_refs = in_refs
            rows_ref[chunk] = wide_ref[0] + arrived_ref[0].astype(F32)
        for i in range(count):
            source = rows_ref.at[chunk, pl.ds(i * size, size), :]
            target = out_ref.at[0, pl.ds(i * stride + chunk * size, size), :]
            copies.append(pltpu.make_async_copy(source, target, sems.at[chunk, i]))
            copies[-1].start()
    for copy in copies:
        copy.wait()


def body(
    temporal,
    frame_ids,
    proj_weight,
    embed_table,
    qkv_weight,
    out_weight,
    gate_up,
    down_weight,
    norm_gains,
):
    hidden_count = lax.axis_size("hidden")
    code_count = lax.axis_size("codebook")
    pair_bit, far_bit = bits_of("hidden")
    code_bits = bits_of("codebook")[::-1]
    width = embed_table.shape[2]
    local_width = qkv_weight.shape[3]
    head_size = width // HEADS

    block_rows = temporal.shape[0]
    size = block_rows // CHUNKS
    rows = code_count * size
    row_count = code_count * block_rows
    split = block_rows // SPLITS
    pieces = [slots_of(temporal[i * split : (i + 1) * split], "codebook") for i in range(SPLITS)]
    earlier = shifted(frame_ids.reshape(code_count, -1), "codebook", 1)
    step = Steps()
    wide, sent = ((rows, width), F32), ((rows, width), BF16)
    states = [{} for _ in range(CHUNKS)]

    def get(c):
        return states[c] if 0 <= c < CHUNKS else None

    def project(c):
        if (s := get(c)) is not None:
            s["part"] = step(
                functools.partial(proj_kernel, c * size % split),
                "project",
                [wide],
                [*pieces[c * size // split], proj_weight],
                [pltpu.VMEM((rows, temporal.shape[1]), BF16)],
            )[0]

    def embed(c):
        if (s := get(c)) is not None:
            s["embedded"] = step(
                functools.partial(embed_kernel, c), "embed", [sent], [earlier, embed_table]
            )[0]

    def exchange(t):
        giver = get(t) if get(t) is not None else get(t - 4)
        name = "part"
        if giver is None and get(t - 8) is not None and get(t - 6) is not None:
            giver, name = get(t - 8), "sums_sent"
        early = get(t - 2)
        taker = early if early is not None else get(t - 6)
        if giver is None and taker is None:
            return
        names = ["total", "far", "embedded"] if early is not None else ["x_zero", "total", "far"]
        parts = [giver[name]] if giver is not None else []
        terms = [taker[name] for name in names] if taker is not None else []
        *finished, out = step(
            functools.partial(mix_kernel, len(terms)),
            "exchange",
            [wide, sent] if terms else [sent],
            [*parts, *terms],
        )
        arrived = swap(out, "hidden", pair_bit)
        if giver is not None:
            giver["arrived"] = arrived
        if taker is not None:
            done = "x_zero" if early is not None else "residual"
            taker[done], taker[done + "_arrived"] = finished[0], arrived

    def pair_sum(c):
        if (s := get(c)) is not None:
            s["total"], out = step(sum_kernel, "pair_sum", [wide, sent], [s["part"], s["arrived"]])
            s["far"] = middle_swap(out)

    def qkv(c):
        if (s := get(c)) is not None:
            s["query"], kv = step(
                qkv_kernel,
                "qkv",
                [((rows, local_width), BF16), ((2, rows, local_width), BF16)],
                [s["x_zero"], s["x_zero_arrived"], norm_gains, qkv_weight],
                [pltpu.VMEM((rows, width), F32)],
            )
            s["kvs"] = {0: kv} | {bit: swap(kv, "codebook", bit) for bit in code_bits}

    def forward(c):
        if (s := get(c)) is not None:
            for bit in code_bits:
                for slot in [slot for slot in s["kvs"] if slot > bit and not slot & (2 * bit - 1)]:
                    (kv,) = step(pass_kernel, "pass", [((2, rows, local_width), BF16)], [s["kvs"][slot]], aliases={0: 0})
                    s["kvs"][slot ^ bit] = swap(kv, "codebook", bit)

    def attend(c):
        if (s := get(c)) is not None:
            s["part"] = step(
                functools.partial(attend_kernel, head_size),
                "attend",
                [wide],
                [s["query"], *[s["kvs"][slot] for slot in range(code_count)], out_weight],
            )[0]

    def rides(c):
        return c + 8 < CHUNKS + 6

    def mlp(c):
        if (s := get(c)) is not None:
            shape = (rows, width) if rides(c) else (hidden_count // 2, rows, local_width)
            s["sums"], s["sums_sent"] = step(
                functools.partial(mlp_kernel, hidden_count, rides(c)),
                "mlp",
                [(shape, F32), (shape, BF16)],
                [s["residual"], s["residual_arrived"], norm_gains, gate_up, down_weight],
                [pltpu.VMEM((rows, width), F32), pltpu.VMEM((min(rows, 128), gate_up.shape[3]), BF16)],
            )
            if not rides(c):
                s["arrived"] = swap(s["sums_sent"], "hidden", pair_bit)

    def halve(c):
        if (s := get(c)) is not None and not rides(c):
            shape = (hidden_count // 4, rows, local_width)
            s["wide"], out = step(
                halve_kernel, "halve", [(shape, F32), (shape, BF16)], [s["sums"], s["arrived"]]
            )
            s["last"] = swap(out, "hidden", far_bit)

    def collect(c):
        if (s := get(c)) is not None and rides(c):
            shape = (2, rows, local_width)
            s["wide"], out = step(
                gather_kernel, "gather", [(shape, F32), (shape, BF16)], [s["sums"], s["arrived"]]
            )
            s["far"] = middle_swap(out)

    def give_back(c):
        if (s := get(c)) is not None and rides(c):
            shape = (rows, local_width)
            s["own"], out = step(
                return_kernel, "return", [(shape, F32), (shape, BF16)], [s["wide"], s["far"]]
            )
            s["last"] = swap(out, "hidden", pair_bit)

    def final():
        routes = [rides(c) for c in range(CHUNKS)]
        args = []
        for s, ridden in zip(states, routes):
            args += [s[name] for name in (("own", "sums", "last") if ridden else ("wide", "last"))]
        return step(
            functools.partial(final_kernel, code_count, routes),
            "final",
            [((1, row_count, local_width), F32)],
            args,
            [pltpu.VMEM((CHUNKS, rows, local_width), F32), pltpu.SemaphoreType.DMA((CHUNKS, code_count))],
            out_space=pl.ANY,
        )[0]

    stages = 9
    project(0)
    for t in range(CHUNKS + stages - 1):
        pair_sum(t - 1)
        pair_sum(t - 5)
        exchange(t)
        qkv(t - 3)
        mlp(t - 7)
        collect(t - 9)
        give_back(t - 10)
        halve(t - 8)
        project(t + 1)
        embed(t - 1)
        forward(t - 3)
        attend(t - 3)
    return final()


def solution(mesh):
    placed = (
        P(("frames", "codebook"), "hidden"),
        P("frames", "codebook"),
        P("codebook", "hidden", None),
        P("codebook", None, None),
        P("codebook", None, None, "hidden"),
        P("codebook", "hidden", None),
        P("codebook", None, None, "hidden"),
        P("codebook", "hidden", None),
        P("codebook", None, None),
    )
    return jax.shard_map(
        body,
        mesh=mesh,
        in_specs=placed,
        out_specs=P("codebook", "frames", "hidden"),
        check_vma=False,
    )
```

```python
import functools
import math

import jax
import jax.numpy as jnp
from jax import lax
from jax.experimental import pallas as pl
from jax.experimental.pallas import tpu as pltpu
from jax.sharding import PartitionSpec as P

HEADS = 16
CHUNKS = 4
F32 = jnp.float32
BF16 = jnp.bfloat16
VMEM = pl.BlockSpec(memory_space=pltpu.VMEM)


def swap(block, axis, distance):
    count = lax.axis_size(axis)
    return lax.ppermute(block, axis, [(i, i ^ distance) for i in range(count)])


def middle_swap(block):
    ends, codes = lax.axis_size("hidden"), lax.axis_size("codebook")
    route = []
    for code in range(codes):
        for i in range(ends):
            other = (code, ends - 1 - i) if 0 < i < ends - 1 else (code ^ 1, i)
            route.append((code * ends + i, other[0] * ends + other[1]))
    return lax.ppermute(block, ("codebook", "hidden"), route)


def is_middle():
    index = lax.axis_index("hidden")
    return (index > 0) & (index < lax.axis_size("hidden") - 1)


def bits_of(axis):
    count = lax.axis_size(axis)
    return [1 << b for b in range(count.bit_length() - 1)]


def shifted(block, axis, distance):
    devices = range(lax.axis_size(axis))
    route = [(i - distance, i) for i in devices if i - distance in devices]
    return lax.ppermute(block, axis, route)


def slots_of(block, axis):
    slots = {0: block}
    for bit in reversed(bits_of(axis)):
        slots.update({slot ^ bit: swap(piece, axis, bit) for slot, piece in slots.items()})
    return [slots[slot] for slot in range(len(slots))]


def dot(a, b):
    return jnp.dot(a, b, preferred_element_type=F32)


def normalize(values, norm_gain):
    return values * lax.rsqrt(jnp.mean(values * values, axis=-1, keepdims=True) + 1e-05) * norm_gain


class Steps:
    def __init__(self):
        self.token = None

    def __call__(self, kernel, name, outs, args, scratch=(), aliases=None, out_space=pltpu.VMEM):
        tokens = [] if self.token is None else [self.token]
        count, given = len(outs), len(args)
        held = [(a.shape, a.dtype) for a in args] + list(outs)
        size = sum(math.prod(shape) * jnp.dtype(dtype).itemsize for shape, dtype in held)

        def with_token(*refs):
            inputs, rest = refs[:given], refs[given + len(tokens) :]
            outputs, token_ref, scratches = rest[:count], rest[count], rest[count + 1 :]
            kernel(*inputs, *outputs, *scratches)
            token_ref[...] = jnp.zeros_like(token_ref)

        *results, self.token = pl.pallas_call(
            with_token,
            name=name,
            out_shape=[jax.ShapeDtypeStruct(shape, dtype) for shape, dtype in outs]
            + [jax.ShapeDtypeStruct((8, 128), F32)],
            in_specs=[VMEM] * (given + len(tokens)),
            out_specs=[pl.BlockSpec(memory_space=out_space)] * count + [VMEM],
            scratch_shapes=list(scratch),
            input_output_aliases=aliases or {},
            cost_estimate=pl.CostEstimate(flops=1000, bytes_accessed=1000, transcendentals=0),
            compiler_params=pltpu.CompilerParams(vmem_limit_bytes=size + (6 << 20)),
        )(*args, *tokens)
        return results


def load(array):
    def kernel(array_ref, out_ref, sem):
        copy = pltpu.make_async_copy(array_ref, out_ref, sem)
        copy.start()
        copy.wait()

    return pl.pallas_call(
        kernel,
        name="load",
        out_shape=pltpu.VMEM(array.shape, array.dtype),
        in_specs=[pl.BlockSpec(memory_space=pltpu.HBM)],
        out_specs=VMEM,
        scratch_shapes=[pltpu.SemaphoreType.DMA],
        cost_estimate=pl.CostEstimate(flops=1000, bytes_accessed=1 << 24, transcendentals=0),
        compiler_params=pltpu.CompilerParams(vmem_limit_bytes=math.prod(array.shape) * 2 + (6 << 20)),
    )(array)


def row_blocks(rows):
    size = min(rows, 128)
    return [pl.ds(start, size) for start in range(0, rows, size)]


def proj_kernel(start, *refs):
    *piece_refs, weight_ref, out_ref, rows_ref = refs
    code = lax.axis_index("codebook")
    size = rows_ref.shape[0] // len(piece_refs)
    for i in range(len(piece_refs)):
        for slot, piece_ref in enumerate(piece_refs):

            @pl.when(code ^ i == slot)
            def _():
                rows_ref[i * size : (i + 1) * size, :] = piece_ref[start : start + size, :]

    for block in row_blocks(rows_ref.shape[0]):
        out_ref[block, :] = dot(rows_ref[block, :], weight_ref[0])


def embed_kernel(chunk, ids_ref, table_ref, out_ref):
    first = lax.axis_index("codebook") == 0
    start_id = table_ref.shape[1] - 1
    count, length = ids_ref.shape
    size = out_ref.shape[0] // count
    diagonal = lax.broadcasted_iota(jnp.int32, (length, length), 0) == lax.broadcasted_iota(
        jnp.int32, (length, length), 1
    )
    columns = []
    for i in range(count):
        line = ids_ref[i : i + 1, :].astype(F32)
        column = jnp.sum(jnp.where(diagonal, line, 0.0), axis=1, keepdims=True).astype(jnp.int32)
        columns.append(column[chunk * size : (chunk + 1) * size])
    all_ids = jnp.where(first, start_id, jnp.concatenate(columns, axis=0))
    for block in row_blocks(out_ref.shape[0]):
        ids = all_ids[block.start : block.start + block.size]
        token = lax.broadcasted_iota(jnp.int32, (block.size, start_id), 1)
        chosen = (token == ids).astype(F32).astype(BF16)
        started = jnp.where(ids == start_id, 1.0, 0.0) * table_ref[0, start_id:, :].astype(F32)
        out_ref[block, :] = (dot(chosen, table_ref[0, :start_id, :]) + started).astype(BF16)


def sum_kernel(*refs):
    *term_refs, wide_ref, sent_ref = refs
    total = term_refs[0][...].astype(F32)
    for term_ref in term_refs[1:]:
        total = total + term_ref[...].astype(F32)
    wide_ref[...] = total
    sent_ref[...] = total.astype(BF16)


def pass_kernel(given_ref, taken_ref):
    pass


def mix_kernel(terms, *refs):
    outs = 2 if terms else 1
    sent_ref = refs[-1]
    part_refs, term_refs = refs[: len(refs) - outs - terms], refs[len(refs) - outs - terms : -outs]

    def send_part():
        sent_ref[...] = part_refs[0][...].astype(BF16)

    def send_rows():
        total = term_refs[0][...].astype(F32)
        for term_ref in term_refs[1:]:
            total = total + term_ref[...].astype(F32)
        refs[-2][...] = total
        sent_ref[...] = total.astype(BF16)

    if not term_refs:
        send_part()
    elif not part_refs:
        send_rows()
    else:
        pl.when(is_middle())(send_rows)
        pl.when(jnp.logical_not(is_middle()))(send_part)


def choose(wide_ref, arrived_ref, rows_ref):
    @pl.when(is_middle())
    def _():
        rows_ref[...] = wide_ref[...]

    @pl.when(jnp.logical_not(is_middle()))
    def _():
        rows_ref[...] = arrived_ref[...].astype(F32)


def qkv_kernel(wide_ref, arrived_ref, gain_ref, weight_ref, query_ref, kv_ref, rows_ref):
    choose(wide_ref, arrived_ref, rows_ref)
    for block in row_blocks(rows_ref.shape[0]):
        normed = normalize(rows_ref[block, :].astype(F32), gain_ref[0, 0:1, :]).astype(BF16)
        query_ref[block, :] = dot(normed, weight_ref[0, 0]).astype(BF16)
        kv_ref[0, block, :] = dot(normed, weight_ref[0, 1]).astype(BF16)
        kv_ref[1, block, :] = dot(normed, weight_ref[0, 2]).astype(BF16)


def attend_kernel(head_size, query_ref, *refs):
    *kv_refs, weight_ref, part_ref = refs
    code = lax.axis_index("codebook")
    width = query_ref.shape[-1]
    lanes = 128
    column = lax.broadcasted_iota(jnp.int32, (width, lanes), 0) // head_size
    head = lax.broadcasted_iota(jnp.int32, (width, lanes), 1)
    gather = (column == head).astype(F32).astype(BF16)
    head_t = lax.broadcasted_iota(jnp.int32, (lanes, width), 0)
    column_t = lax.broadcasted_iota(jnp.int32, (lanes, width), 1) // head_size
    spread = (column_t == head_t).astype(F32).astype(BF16)
    for block in row_blocks(query_ref.shape[0]):
        query = query_ref[block, :].astype(F32)
        scores = []
        for slot, kv_ref in enumerate(kv_refs):
            product = query * kv_ref[0, block, :].astype(F32)
            high = product.astype(BF16)
            low = (product - high.astype(F32)).astype(BF16)
            score = (dot(high, gather) + dot(low, gather)) * head_size ** (-0.5)
            if slot:
                score = jnp.where((code ^ slot) <= code, score, -1e30)
            scores.append(score)
        highest = functools.reduce(jnp.maximum, scores)
        weights = [jnp.exp(score - highest) for score in scores]
        running = functools.reduce(jnp.add, weights)
        summed = None
        for kv_ref, weight in zip(kv_refs, weights):
            term = dot(weight.astype(BF16), spread) * kv_ref[1, block, :].astype(F32)
            summed = term if summed is None else summed + term
        inverse = 1.0 / running
        high = inverse.astype(BF16)
        low = (inverse - high.astype(F32)).astype(BF16)
        attended = (summed * (dot(high, spread) + dot(low, spread))).astype(BF16)
        part_ref[block, :] = dot(attended, weight_ref[0]).astype(part_ref.dtype)


def mlp_kernel(count, form, wide_ref, arrived_ref, gain_ref, gate_up_ref, down_ref, *refs):
    kept_ref, *sent_refs, rows_ref, act_ref = refs
    sent_ref = sent_refs[0]
    choose(wide_ref, arrived_ref, rows_ref)
    index = lax.axis_index("hidden")
    hidden = act_ref.shape[1]
    step = min(hidden, 256)
    width = down_ref.shape[2] // count
    own = pl.ds(pl.multiple_of(index * width, width), width)
    for block in row_blocks(rows_ref.shape[0]):
        normed = normalize(rows_ref[block, :], gain_ref[0, 1:2, :]).astype(BF16)
        for start in range(0, hidden, step):
            columns = pl.ds(start, step)
            gate_sum = dot(normed, gate_up_ref[0, 0, :, columns])
            upper_sum = dot(normed, gate_up_ref[0, 1, :, columns])
            act_ref[:, columns] = (jax.nn.silu(gate_sum) * upper_sum).astype(BF16)
        if form == "direct":
            for i in reversed(range(count)):
                owner = index ^ i
                columns = pl.ds(pl.multiple_of(owner * width, width), width)
                total = dot(act_ref[...], down_ref[0, :, columns])
                if i:
                    sent_refs[i - 1][block, :] = total.astype(BF16)
                else:
                    kept_ref[block, :] = total + rows_ref[block, columns]
            continue
        if form == "whole":
            total = dot(act_ref[...], down_ref[0])
            sent_ref[block, :] = total.astype(BF16)
            kept_ref[block, :] = total
            kept_ref[block, own] = kept_ref[block, own] + rows_ref[block, own]
            continue
        for i in range(count // 2):
            owner = index ^ (2 * i)
            columns = pl.ds(pl.multiple_of((owner ^ 1) * width, width), width)
            sent_ref[i, block, :] = dot(act_ref[...], down_ref[0, :, columns]).astype(BF16)
        for i in range(count // 2):
            owner = index ^ (2 * i)
            columns = pl.ds(pl.multiple_of(owner * width, width), width)
            total = dot(act_ref[...], down_ref[0, :, columns])
            if i == 0:
                total = total + rows_ref[block, columns]
            kept_ref[i, block, :] = total


def gather_kernel(mine_ref, arrived_ref, wide_ref, sent_ref):
    index = lax.axis_index("hidden")
    width = wide_ref.shape[2]
    far = lax.axis_size("hidden") - 1 - index

    def columns(owner):
        return pl.ds(pl.multiple_of(owner * width, width), width)

    def total(owner):
        return mine_ref[:, columns(owner)] + arrived_ref[:, columns(owner)].astype(F32)

    wide_ref[0] = total(index)
    wide_ref[1] = mine_ref[:, columns(index ^ 1)]
    sent_ref[0] = total(far).astype(BF16)
    sent_ref[1] = total(far ^ 1).astype(BF16)


def return_kernel(wide_ref, arrived_ref, own_ref, sent_ref):
    own_ref[...] = wide_ref[0] + arrived_ref[0].astype(F32)
    sent_ref[...] = (wide_ref[1] + arrived_ref[1].astype(F32)).astype(BF16)


def halve_kernel(mine_ref, arrived_ref, wide_ref, sent_ref):
    kept = wide_ref.shape[0]
    wide_ref[...] = mine_ref[:kept] + arrived_ref[:kept].astype(F32)
    sent_ref[...] = (mine_ref[kept:] + arrived_ref[kept:].astype(F32)).astype(BF16)


def final_kernel(count, forms, *refs):
    *in_refs, out_ref, rows_ref, sems = refs
    chunks = rows_ref.shape[0]
    stride = out_ref.shape[1] // count
    size = stride // chunks
    width = out_ref.shape[2]
    index = lax.axis_index("hidden")
    copies = []
    for chunk in range(chunks):
        if forms[chunk] == "direct":
            total_ref, *in_refs = in_refs
            total = total_ref[...]
            for arrived_ref in in_refs:
                total = total + arrived_ref[...].astype(F32)
            rows_ref[chunk] = total
        elif forms[chunk] == "whole":
            own_ref, mine_ref, arrived_ref, *in_refs = in_refs

            @pl.when(is_middle())
            def _():
                rows_ref[chunk] = own_ref[...]

            @pl.when(jnp.logical_not(is_middle()))
            def _():
                mine = mine_ref[:, pl.ds(pl.multiple_of(index * width, width), width)]
                rows_ref[chunk] = mine + arrived_ref[...].astype(F32)

        else:
            wide_ref, arrived_ref, *in_refs = in_refs
            rows_ref[chunk] = wide_ref[0] + arrived_ref[0].astype(F32)
        for i in range(count):
            source = rows_ref.at[chunk, pl.ds(i * size, size), :]
            target = out_ref.at[0, pl.ds(i * stride + chunk * size, size), :]
            copies.append(pltpu.make_async_copy(source, target, sems.at[chunk, i]))
            copies[-1].start()
    for copy in copies:
        copy.wait()


def body(
    temporal,
    frame_ids,
    proj_weight,
    embed_table,
    qkv_weight,
    out_weight,
    gate_up,
    down_weight,
    norm_gains,
):
    hidden_count = lax.axis_size("hidden")
    code_count = lax.axis_size("codebook")
    pair_bit, far_bit = bits_of("hidden")
    code_bits = bits_of("codebook")[::-1]
    width = embed_table.shape[2]
    local_width = qkv_weight.shape[3]
    head_size = width // HEADS

    block_rows = temporal.shape[0]
    size = block_rows // CHUNKS
    rows = code_count * size
    row_count = code_count * block_rows
    pieces = [slots_of(part, "codebook") for part in (temporal[:size], temporal[size:])]
    earlier = shifted(frame_ids.reshape(code_count, -1), "codebook", 1)
    step = Steps()
    wide, sent = ((rows, width), F32), ((rows, width), BF16)
    states = [{} for _ in range(CHUNKS)]

    def get(c):
        return states[c] if 0 <= c < CHUNKS else None

    def project(c):
        if (s := get(c)) is not None:
            s["part"] = step(
                functools.partial(proj_kernel, max(c - 1, 0) * size),
                "project",
                [wide],
                [*pieces[min(c, 1)], proj_weight],
                [pltpu.VMEM((rows, temporal.shape[1]), BF16)],
            )[0]

    def embed(c):
        if (s := get(c)) is not None:
            s["embedded"] = step(
                functools.partial(embed_kernel, c), "embed", [sent], [earlier, embed_table]
            )[0]

    def exchange(t):
        giver = get(t) if get(t) is not None else get(t - 4)
        name = "part"
        if giver is None and get(t - 8) is not None and get(t - 6) is not None:
            giver, name = get(t - 8), "sums_sent"
        early = get(t - 2)
        taker = early if early is not None else get(t - 6)
        if giver is None and taker is None:
            return
        names = ["total", "far", "embedded"] if early is not None else ["x_zero", "total", "far"]
        parts = [giver[name]] if giver is not None else []
        terms = [taker[name] for name in names] if taker is not None else []
        *finished, out = step(
            functools.partial(mix_kernel, len(terms)),
            "exchange",
            [wide, sent] if terms else [sent],
            [*parts, *terms],
        )
        arrived = swap(out, "hidden", pair_bit)
        if giver is not None:
            giver["arrived"] = arrived
        if taker is not None:
            done = "x_zero" if early is not None else "residual"
            taker[done], taker[done + "_arrived"] = finished[0], arrived

    def pair_sum(c):
        if (s := get(c)) is not None:
            s["total"], out = step(sum_kernel, "pair_sum", [wide, sent], [s["part"], s["arrived"]])
            s["far"] = middle_swap(out)

    def qkv(c):
        if (s := get(c)) is not None:
            s["query"], kv = step(
                qkv_kernel,
                "qkv",
                [((rows, local_width), BF16), ((2, rows, local_width), BF16)],
                [s["x_zero"], s["x_zero_arrived"], norm_gains, qkv_weight],
                [pltpu.VMEM((rows, width), F32)],
            )
            s["kvs"] = {0: kv} | {bit: swap(kv, "codebook", bit) for bit in code_bits}

    def forward(c):
        if (s := get(c)) is not None:
            for bit in code_bits:
                for slot in [slot for slot in s["kvs"] if slot > bit and not slot & (2 * bit - 1)]:
                    (kv,) = step(pass_kernel, "pass", [((2, rows, local_width), BF16)], [s["kvs"][slot]], aliases={0: 0})
                    s["kvs"][slot ^ bit] = swap(kv, "codebook", bit)

    def attend(c):
        if (s := get(c)) is not None:
            s["part"] = step(
                functools.partial(attend_kernel, head_size),
                "attend",
                [wide],
                [s["query"], *[s["kvs"][slot] for slot in range(code_count)], out_weight],
            )[0]

    def form(c):
        if c + 8 < CHUNKS + 6:
            return "whole"
        return "direct" if c == CHUNKS - 1 else "halves"

    def mlp(c):
        if (s := get(c)) is not None:
            shape = {
                "whole": (rows, width),
                "halves": (hidden_count // 2, rows, local_width),
                "direct": (rows, local_width),
            }[form(c)]
            messages = hidden_count - 1 if form(c) == "direct" else 1
            s["sums"], s["sums_sent"], *others = step(
                functools.partial(mlp_kernel, hidden_count, form(c)),
                "mlp",
                [(shape, F32)] + [(shape, BF16)] * messages,
                [s["residual"], s["residual_arrived"], norm_gains, gate_up, down_weight],
                [pltpu.VMEM((rows, width), F32), pltpu.VMEM((min(rows, 128), gate_up.shape[3]), BF16)],
            )
            if form(c) == "halves":
                s["arrived"] = swap(s["sums_sent"], "hidden", pair_bit)
            if form(c) == "direct":
                others = [s["sums_sent"], *others]
                s["direct"] = [swap(out, "hidden", i + 1) for i, out in reversed(list(enumerate(others)))]

    def halve(c):
        if (s := get(c)) is not None and form(c) == "halves":
            shape = (hidden_count // 4, rows, local_width)
            s["wide"], out = step(
                halve_kernel, "halve", [(shape, F32), (shape, BF16)], [s["sums"], s["arrived"]]
            )
            s["last"] = swap(out, "hidden", far_bit)

    def collect(c):
        if (s := get(c)) is not None and form(c) == "whole":
            shape = (2, rows, local_width)
            s["wide"], out = step(
                gather_kernel, "gather", [(shape, F32), (shape, BF16)], [s["sums"], s["arrived"]]
            )
            s["far"] = middle_swap(out)

    def give_back(c):
        if (s := get(c)) is not None and form(c) == "whole":
            shape = (rows, local_width)
            s["own"], out = step(
                return_kernel, "return", [(shape, F32), (shape, BF16)], [s["wide"], s["far"]]
            )
            s["last"] = swap(out, "hidden", pair_bit)

    def final():
        forms = [form(c) for c in range(CHUNKS)]
        args = []
        for s, kind in zip(states, forms):
            names = {"whole": ("own", "sums", "last"), "halves": ("wide", "last"), "direct": ("sums",)}[kind]
            args += [s[name] for name in names] + s.get("direct", [])
        return step(
            functools.partial(final_kernel, code_count, forms),
            "final",
            [((1, row_count, local_width), F32)],
            args,
            [pltpu.VMEM((CHUNKS, rows, local_width), F32), pltpu.SemaphoreType.DMA((CHUNKS, code_count))],
            out_space=pl.ANY,
        )[0]

    stages = 9
    project(0)
    for t in range(CHUNKS + stages - 1):
        pair_sum(t - 1)
        pair_sum(t - 5)
        exchange(t)
        qkv(t - 3)
        collect(t - 9)
        give_back(t - 10)
        mlp(t - 7)
        halve(t - 8)
        project(t + 1)
        embed(t - 1)
        forward(t - 3)
        attend(t - 3)
    return final()


def solution(mesh):
    placed = (
        P(("frames", "codebook"), "hidden"),
        P("frames", "codebook"),
        P("codebook", "hidden", None),
        P("codebook", None, None),
        P("codebook", None, None, "hidden"),
        P("codebook", "hidden", None),
        P("codebook", None, None, "hidden"),
        P("codebook", "hidden", None),
        P("codebook", None, None),
    )
    return jax.shard_map(
        body,
        mesh=mesh,
        in_specs=placed,
        out_specs=P("codebook", "frames", "hidden"),
        check_vma=False,
    )
```

```python
import functools
import math

import jax
import jax.numpy as jnp
from jax import lax
from jax.experimental import pallas as pl
from jax.experimental.pallas import tpu as pltpu
from jax.sharding import PartitionSpec as P

HEADS = 16
CHUNKS = 4
F32 = jnp.float32
BF16 = jnp.bfloat16
VMEM = pl.BlockSpec(memory_space=pltpu.VMEM)


def swap(block, axis, distance):
    count = lax.axis_size(axis)
    return lax.ppermute(block, axis, [(i, i ^ distance) for i in range(count)])


def middle_swap(block):
    ends, codes = lax.axis_size("hidden"), lax.axis_size("codebook")
    route = []
    for code in range(codes):
        for i in range(ends):
            other = (code, ends - 1 - i) if 0 < i < ends - 1 else (code ^ 1, i)
            route.append((code * ends + i, other[0] * ends + other[1]))
    return lax.ppermute(block, ("codebook", "hidden"), route)


def is_middle():
    index = lax.axis_index("hidden")
    return (index > 0) & (index < lax.axis_size("hidden") - 1)


def bits_of(axis):
    count = lax.axis_size(axis)
    return [1 << b for b in range(count.bit_length() - 1)]


def shifted(block, axis, distance):
    devices = range(lax.axis_size(axis))
    route = [(i - distance, i) for i in devices if i - distance in devices]
    return lax.ppermute(block, axis, route)


def slots_of(block, axis):
    slots = {0: block}
    for bit in reversed(bits_of(axis)):
        slots.update({slot ^ bit: swap(piece, axis, bit) for slot, piece in slots.items()})
    return [slots[slot] for slot in range(len(slots))]


def dot(a, b):
    return jnp.dot(a, b, preferred_element_type=F32)


def normalize(values, norm_gain):
    return values * lax.rsqrt(jnp.mean(values * values, axis=-1, keepdims=True) + 1e-05) * norm_gain


class Steps:
    def __init__(self):
        self.token = None

    def __call__(self, kernel, name, outs, args, scratch=(), aliases=None, out_space=pltpu.VMEM):
        tokens = [] if self.token is None else [self.token]
        count, given = len(outs), len(args)
        held = [(a.shape, a.dtype) for a in args] + list(outs)
        size = sum(math.prod(shape) * jnp.dtype(dtype).itemsize for shape, dtype in held)

        def with_token(*refs):
            inputs, rest = refs[:given], refs[given + len(tokens) :]
            outputs, token_ref, scratches = rest[:count], rest[count], rest[count + 1 :]
            kernel(*inputs, *outputs, *scratches)
            token_ref[...] = jnp.zeros_like(token_ref)

        *results, self.token = pl.pallas_call(
            with_token,
            name=name,
            out_shape=[jax.ShapeDtypeStruct(shape, dtype) for shape, dtype in outs]
            + [jax.ShapeDtypeStruct((8, 128), F32)],
            in_specs=[VMEM] * (given + len(tokens)),
            out_specs=[pl.BlockSpec(memory_space=out_space)] * count + [VMEM],
            scratch_shapes=list(scratch),
            input_output_aliases=aliases or {},
            cost_estimate=pl.CostEstimate(flops=1000, bytes_accessed=1000, transcendentals=0),
            compiler_params=pltpu.CompilerParams(vmem_limit_bytes=size + (6 << 20)),
        )(*args, *tokens)
        return results


def load(array):
    def kernel(array_ref, out_ref, sem):
        copy = pltpu.make_async_copy(array_ref, out_ref, sem)
        copy.start()
        copy.wait()

    return pl.pallas_call(
        kernel,
        name="load",
        out_shape=pltpu.VMEM(array.shape, array.dtype),
        in_specs=[pl.BlockSpec(memory_space=pltpu.HBM)],
        out_specs=VMEM,
        scratch_shapes=[pltpu.SemaphoreType.DMA],
        cost_estimate=pl.CostEstimate(flops=1000, bytes_accessed=1 << 24, transcendentals=0),
        compiler_params=pltpu.CompilerParams(vmem_limit_bytes=math.prod(array.shape) * 2 + (6 << 20)),
    )(array)


def row_blocks(rows):
    size = min(rows, 128)
    return [pl.ds(start, size) for start in range(0, rows, size)]


def proj_kernel(start, *refs):
    *piece_refs, weight_ref, out_ref, rows_ref = refs
    code = lax.axis_index("codebook")
    size = rows_ref.shape[0] // len(piece_refs)
    for i in range(len(piece_refs)):
        for slot, piece_ref in enumerate(piece_refs):

            @pl.when(code ^ i == slot)
            def _():
                rows_ref[i * size : (i + 1) * size, :] = piece_ref[start : start + size, :]

    for block in row_blocks(rows_ref.shape[0]):
        out_ref[block, :] = dot(rows_ref[block, :], weight_ref[0])


def embed_kernel(chunk, ids_ref, table_ref, out_ref):
    first = lax.axis_index("codebook") == 0
    start_id = table_ref.shape[1] - 1
    count, length = ids_ref.shape
    size = out_ref.shape[0] // count
    diagonal = lax.broadcasted_iota(jnp.int32, (length, length), 0) == lax.broadcasted_iota(
        jnp.int32, (length, length), 1
    )
    columns = []
    for i in range(count):
        line = ids_ref[i : i + 1, :].astype(F32)
        column = jnp.sum(jnp.where(diagonal, line, 0.0), axis=1, keepdims=True).astype(jnp.int32)
        columns.append(column[chunk * size : (chunk + 1) * size])
    all_ids = jnp.where(first, start_id, jnp.concatenate(columns, axis=0))
    for block in row_blocks(out_ref.shape[0]):
        ids = all_ids[block.start : block.start + block.size]
        token = lax.broadcasted_iota(jnp.int32, (block.size, start_id), 1)
        chosen = (token == ids).astype(F32).astype(BF16)
        started = jnp.where(ids == start_id, 1.0, 0.0) * table_ref[0, start_id:, :].astype(F32)
        out_ref[block, :] = (dot(chosen, table_ref[0, :start_id, :]) + started).astype(BF16)


def sum_kernel(*refs):
    *term_refs, wide_ref, sent_ref = refs
    total = term_refs[0][...].astype(F32)
    for term_ref in term_refs[1:]:
        total = total + term_ref[...].astype(F32)
    wide_ref[...] = total
    sent_ref[...] = total.astype(BF16)


def pass_kernel(given_ref, taken_ref):
    pass


def mix_kernel(terms, *refs):
    outs = 2 if terms else 1
    sent_ref = refs[-1]
    part_refs, term_refs = refs[: len(refs) - outs - terms], refs[len(refs) - outs - terms : -outs]

    def send_part():
        sent_ref[...] = part_refs[0][...].astype(BF16)

    def send_rows():
        total = term_refs[0][...].astype(F32)
        for term_ref in term_refs[1:]:
            total = total + term_ref[...].astype(F32)
        refs[-2][...] = total
        sent_ref[...] = total.astype(BF16)

    if not term_refs:
        send_part()
    elif not part_refs:
        send_rows()
    else:
        pl.when(is_middle())(send_rows)
        pl.when(jnp.logical_not(is_middle()))(send_part)


def choose(wide_ref, arrived_ref, block):
    return jnp.where(is_middle(), wide_ref[block, :], arrived_ref[block, :].astype(F32))


def qkv_kernel(wide_ref, arrived_ref, gain_ref, weight_ref, query_ref, kv_ref):
    for block in row_blocks(wide_ref.shape[0]):
        rows = choose(wide_ref, arrived_ref, block)
        normed = normalize(rows, gain_ref[0, 0:1, :]).astype(BF16)
        query_ref[block, :] = dot(normed, weight_ref[0, 0]).astype(BF16)
        kv_ref[0, block, :] = dot(normed, weight_ref[0, 1]).astype(BF16)
        kv_ref[1, block, :] = dot(normed, weight_ref[0, 2]).astype(BF16)


def attend_kernel(head_size, query_ref, *refs):
    *kv_refs, weight_ref, part_ref = refs
    code = lax.axis_index("codebook")
    width = query_ref.shape[-1]
    lanes = 128
    column = lax.broadcasted_iota(jnp.int32, (width, lanes), 0) // head_size
    head = lax.broadcasted_iota(jnp.int32, (width, lanes), 1)
    gather = (column == head).astype(F32).astype(BF16)
    head_t = lax.broadcasted_iota(jnp.int32, (lanes, width), 0)
    column_t = lax.broadcasted_iota(jnp.int32, (lanes, width), 1) // head_size
    spread = (column_t == head_t).astype(F32).astype(BF16)
    for block in row_blocks(query_ref.shape[0]):
        query = query_ref[block, :].astype(F32)
        scores = []
        for slot, kv_ref in enumerate(kv_refs):
            product = query * kv_ref[0, block, :].astype(F32)
            high = product.astype(BF16)
            low = (product - high.astype(F32)).astype(BF16)
            score = (dot(high, gather) + dot(low, gather)) * head_size ** (-0.5)
            if slot:
                score = jnp.where((code ^ slot) <= code, score, -1e30)
            scores.append(score)
        highest = functools.reduce(jnp.maximum, scores)
        weights = [jnp.exp(score - highest) for score in scores]
        running = functools.reduce(jnp.add, weights)
        summed = None
        for kv_ref, weight in zip(kv_refs, weights):
            term = dot(weight.astype(BF16), spread) * kv_ref[1, block, :].astype(F32)
            summed = term if summed is None else summed + term
        inverse = 1.0 / running
        high = inverse.astype(BF16)
        low = (inverse - high.astype(F32)).astype(BF16)
        attended = (summed * (dot(high, spread) + dot(low, spread))).astype(BF16)
        part_ref[block, :] = dot(attended, weight_ref[0]).astype(part_ref.dtype)


def mlp_kernel(count, form, wide_ref, arrived_ref, gain_ref, gate_up_ref, down_ref, *refs):
    kept_ref, *sent_refs, act_ref = refs
    sent_ref = sent_refs[0]
    index = lax.axis_index("hidden")
    hidden = act_ref.shape[1]
    step = min(hidden, 256)
    width = down_ref.shape[2] // count
    own = pl.ds(pl.multiple_of(index * width, width), width)
    for block in row_blocks(wide_ref.shape[0]):
        normed = normalize(choose(wide_ref, arrived_ref, block), gain_ref[0, 1:2, :]).astype(BF16)
        residual = jnp.where(is_middle(), wide_ref[block, own], arrived_ref[block, own].astype(F32))
        for start in range(0, hidden, step):
            columns = pl.ds(start, step)
            gate_sum = dot(normed, gate_up_ref[0, 0, :, columns])
            upper_sum = dot(normed, gate_up_ref[0, 1, :, columns])
            act_ref[:, columns] = (jax.nn.silu(gate_sum) * upper_sum).astype(BF16)
        if form == "direct":
            for i in reversed(range(count)):
                owner = index ^ i
                columns = pl.ds(pl.multiple_of(owner * width, width), width)
                total = dot(act_ref[...], down_ref[0, :, columns])
                if i:
                    sent_refs[i - 1][block, :] = total.astype(BF16)
                else:
                    kept_ref[block, :] = total + residual
            continue
        if form == "whole":
            total = dot(act_ref[...], down_ref[0])
            sent_ref[block, :] = total.astype(BF16)
            kept_ref[block, :] = total
            kept_ref[block, own] = kept_ref[block, own] + residual
            sent_refs[1][block, :] = kept_ref[block, own]
            continue
        for i in range(count // 2):
            owner = index ^ (2 * i)
            columns = pl.ds(pl.multiple_of((owner ^ 1) * width, width), width)
            sent_ref[i, block, :] = dot(act_ref[...], down_ref[0, :, columns]).astype(BF16)
        for i in range(count // 2):
            owner = index ^ (2 * i)
            columns = pl.ds(pl.multiple_of(owner * width, width), width)
            total = dot(act_ref[...], down_ref[0, :, columns])
            if i == 0:
                total = total + residual
            kept_ref[i, block, :] = total


def gather_kernel(mine_ref, arrived_ref, wide_ref, sent_ref):
    index = lax.axis_index("hidden")
    width = wide_ref.shape[2]
    far = lax.axis_size("hidden") - 1 - index

    def columns(owner):
        return pl.ds(pl.multiple_of(owner * width, width), width)

    def total(owner):
        return mine_ref[:, columns(owner)] + arrived_ref[:, columns(owner)].astype(F32)

    wide_ref[0] = total(index)
    wide_ref[1] = mine_ref[:, columns(index ^ 1)]
    sent_ref[0] = total(far).astype(BF16)
    sent_ref[1] = total(far ^ 1).astype(BF16)


def return_kernel(wide_ref, arrived_ref, own_ref, sent_ref):
    own_ref[...] = wide_ref[0] + arrived_ref[0].astype(F32)
    sent_ref[...] = (wide_ref[1] + arrived_ref[1].astype(F32)).astype(BF16)


def halve_kernel(mine_ref, arrived_ref, wide_ref, sent_ref):
    kept = wide_ref.shape[0]
    wide_ref[...] = mine_ref[:kept] + arrived_ref[:kept].astype(F32)
    sent_ref[...] = (mine_ref[kept:] + arrived_ref[kept:].astype(F32)).astype(BF16)


def final_kernel(forms, *refs):
    *in_refs, out_ref, rows_ref, sems = refs
    chunks, count, size, width = rows_ref.shape
    shape = (count, size, width)
    copies = []
    for chunk in range(chunks):
        if forms[chunk] == "direct":
            total_ref, *in_refs = in_refs
            total = total_ref[...]
            for arrived_ref in in_refs:
                total = total + arrived_ref[...].astype(F32)
            rows_ref[chunk] = total.reshape(shape)
        elif forms[chunk] == "whole":
            own_ref, mine_ref, arrived_ref, *in_refs = in_refs

            @pl.when(is_middle())
            def _():
                rows_ref[chunk] = own_ref[...].reshape(shape)

            @pl.when(jnp.logical_not(is_middle()))
            def _():
                rows_ref[chunk] = (mine_ref[...] + arrived_ref[...].astype(F32)).reshape(shape)

        else:
            wide_ref, arrived_ref, *in_refs = in_refs
            rows_ref[chunk] = (wide_ref[0] + arrived_ref[0].astype(F32)).reshape(shape)
        target = out_ref.at[0, :, pl.ds(chunk * size, size), :]
        copies.append(pltpu.make_async_copy(rows_ref.at[chunk], target, sems.at[chunk]))
        copies[-1].start()
    for copy in copies:
        copy.wait()


def body(
    temporal,
    frame_ids,
    proj_weight,
    embed_table,
    qkv_weight,
    out_weight,
    gate_up,
    down_weight,
    norm_gains,
):
    hidden_count = lax.axis_size("hidden")
    code_count = lax.axis_size("codebook")
    pair_bit, far_bit = bits_of("hidden")
    code_bits = bits_of("codebook")[::-1]
    width = embed_table.shape[2]
    local_width = qkv_weight.shape[3]
    head_size = width // HEADS

    block_rows = temporal.shape[0]
    size = block_rows // CHUNKS
    rows = code_count * size
    row_count = code_count * block_rows
    pieces = [slots_of(part, "codebook") for part in (temporal[:size], temporal[size:])]
    earlier = shifted(frame_ids.reshape(code_count, -1), "codebook", 1)
    step = Steps()
    wide, sent = ((rows, width), F32), ((rows, width), BF16)
    states = [{} for _ in range(CHUNKS)]

    def get(c):
        return states[c] if 0 <= c < CHUNKS else None

    def project(c):
        if (s := get(c)) is not None:
            s["part"] = step(
                functools.partial(proj_kernel, max(c - 1, 0) * size),
                "project",
                [wide],
                [*pieces[min(c, 1)], proj_weight],
                [pltpu.VMEM((rows, temporal.shape[1]), BF16)],
            )[0]

    def embed(c):
        if (s := get(c)) is not None:
            s["embedded"] = step(
                functools.partial(embed_kernel, c), "embed", [sent], [earlier, embed_table]
            )[0]

    def exchange(t):
        giver = get(t) if get(t) is not None else get(t - 4)
        name = "part"
        if giver is None and get(t - 8) is not None and get(t - 6) is not None:
            giver, name = get(t - 8), "sums_sent"
        early = get(t - 2)
        taker = early if early is not None else get(t - 6)
        if giver is None and taker is None:
            return
        names = ["total", "far", "embedded"] if early is not None else ["x_zero", "total", "far"]
        parts = [giver[name]] if giver is not None else []
        terms = [taker[name] for name in names] if taker is not None else []
        *finished, out = step(
            functools.partial(mix_kernel, len(terms)),
            "exchange",
            [wide, sent] if terms else [sent],
            [*parts, *terms],
        )
        arrived = swap(out, "hidden", pair_bit)
        if giver is not None:
            giver["arrived"] = arrived
        if taker is not None:
            done = "x_zero" if early is not None else "residual"
            taker[done], taker[done + "_arrived"] = finished[0], arrived

    def pair_sum(c):
        if (s := get(c)) is not None:
            s["total"], out = step(sum_kernel, "pair_sum", [wide, sent], [s["part"], s["arrived"]])
            s["far"] = middle_swap(out)

    def qkv(c):
        if (s := get(c)) is not None:
            s["query"], kv = step(
                qkv_kernel,
                "qkv",
                [((rows, local_width), BF16), ((2, rows, local_width), BF16)],
                [s["x_zero"], s["x_zero_arrived"], norm_gains, qkv_weight],
            )
            s["kvs"] = {0: kv} | {bit: swap(kv, "codebook", bit) for bit in code_bits}

    def forward(c):
        if (s := get(c)) is not None:
            for bit in code_bits:
                for slot in [slot for slot in s["kvs"] if slot > bit and not slot & (2 * bit - 1)]:
                    (kv,) = step(pass_kernel, "pass", [((2, rows, local_width), BF16)], [s["kvs"][slot]], aliases={0: 0})
                    s["kvs"][slot], s["kvs"][slot ^ bit] = kv, swap(kv, "codebook", bit)

    def attend(c):
        if (s := get(c)) is not None:
            s["part"] = step(
                functools.partial(attend_kernel, head_size),
                "attend",
                [wide],
                [s["query"], *[s["kvs"][slot] for slot in range(code_count)], out_weight],
            )[0]

    def form(c):
        if c + 8 < CHUNKS + 6:
            return "whole"
        return "direct" if c == CHUNKS - 1 else "halves"

    def mlp(c):
        if (s := get(c)) is not None:
            shape = {
                "whole": (rows, width),
                "halves": (hidden_count // 2, rows, local_width),
                "direct": (rows, local_width),
            }[form(c)]
            more = {"whole": [F32], "halves": [], "direct": [BF16] * (hidden_count - 2)}[form(c)]
            s["sums"], s["sums_sent"], *others = step(
                functools.partial(mlp_kernel, hidden_count, form(c)),
                "mlp",
                [(shape, F32), (shape, BF16)] + [((rows, local_width), dtype) for dtype in more],
                [s["residual"], s["residual_arrived"], norm_gains, gate_up, down_weight],
                [pltpu.VMEM((min(rows, 128), gate_up.shape[3]), BF16)],
            )
            if form(c) == "whole":
                s["mine"] = others[0]
            if form(c) == "halves":
                s["arrived"] = swap(s["sums_sent"], "hidden", pair_bit)
            if form(c) == "direct":
                others = [s["sums_sent"], *others]
                s["direct"] = [swap(out, "hidden", i + 1) for i, out in reversed(list(enumerate(others)))]

    def halve(c):
        if (s := get(c)) is not None and form(c) == "halves":
            shape = (hidden_count // 4, rows, local_width)
            s["wide"], out = step(
                halve_kernel, "halve", [(shape, F32), (shape, BF16)], [s["sums"], s["arrived"]]
            )
            s["last"] = swap(out, "hidden", far_bit)

    def collect(c):
        if (s := get(c)) is not None and form(c) == "whole":
            shape = (2, rows, local_width)
            s["wide"], out = step(
                gather_kernel, "gather", [(shape, F32), (shape, BF16)], [s["sums"], s["arrived"]]
            )
            s["far"] = middle_swap(out)

    def give_back(c):
        if (s := get(c)) is not None and form(c) == "whole":
            shape = (rows, local_width)
            s["own"], out = step(
                return_kernel, "return", [(shape, F32), (shape, BF16)], [s["wide"], s["far"]]
            )
            s["last"] = swap(out, "hidden", pair_bit)

    def final():
        forms = [form(c) for c in range(CHUNKS)]
        args = []
        for s, kind in zip(states, forms):
            names = {"whole": ("own", "mine", "last"), "halves": ("wide", "last"), "direct": ("sums",)}[kind]
            args += [s[name] for name in names] + s.get("direct", [])
        out = step(
            functools.partial(final_kernel, forms),
            "final",
            [((1, code_count, block_rows, local_width), F32)],
            args,
            [
                pltpu.VMEM((CHUNKS, code_count, size, local_width), F32),
                pltpu.SemaphoreType.DMA((CHUNKS,)),
            ],
            out_space=pl.ANY,
        )[0]
        return out.reshape(1, row_count, local_width)

    stages = 9
    project(0)
    for t in range(CHUNKS + stages - 1):
        if t < 3:
            exchange(t)
            pair_sum(t - 1)
        else:
            qkv(t - 3)
            pair_sum(t - 1)
            pair_sum(t - 5)
            exchange(t)
        collect(t - 9)
        mlp(t - 7)
        give_back(t - 10)
        halve(t - 8)
        project(t + 1)
        embed(t - 1)
        forward(t - 3)
        attend(t - 3)
    return final()


def solution(mesh):
    placed = (
        P(("frames", "codebook"), "hidden"),
        P("frames", "codebook"),
        P("codebook", "hidden", None),
        P("codebook", None, None),
        P("codebook", None, None, "hidden"),
        P("codebook", "hidden", None),
        P("codebook", None, None, "hidden"),
        P("codebook", "hidden", None),
        P("codebook", None, None),
    )
    return jax.shard_map(
        body,
        mesh=mesh,
        in_specs=placed,
        out_specs=P("codebook", "frames", "hidden"),
        check_vma=False,
    )
```

```python
import functools
import math

import jax
import jax.numpy as jnp
from jax import lax
from jax.experimental import pallas as pl
from jax.experimental.pallas import tpu as pltpu
from jax.sharding import PartitionSpec as P

HEADS = 16
CHUNKS = 4
F32 = jnp.float32
BF16 = jnp.bfloat16
VMEM = pl.BlockSpec(memory_space=pltpu.VMEM)


def swap(block, axis, distance):
    count = lax.axis_size(axis)
    return lax.ppermute(block, axis, [(i, i ^ distance) for i in range(count)])


def middle_swap(block):
    ends, codes = lax.axis_size("hidden"), lax.axis_size("codebook")
    route = []
    for code in range(codes):
        for i in range(ends):
            other = (code, ends - 1 - i) if 0 < i < ends - 1 else (code ^ 1, i)
            route.append((code * ends + i, other[0] * ends + other[1]))
    return lax.ppermute(block, ("codebook", "hidden"), route)


def is_middle():
    index = lax.axis_index("hidden")
    return (index > 0) & (index < lax.axis_size("hidden") - 1)


def bits_of(axis):
    count = lax.axis_size(axis)
    return [1 << b for b in range(count.bit_length() - 1)]


def shifted(block, axis, distance):
    devices = range(lax.axis_size(axis))
    route = [(i - distance, i) for i in devices if i - distance in devices]
    return lax.ppermute(block, axis, route)


def slots_of(block, axis):
    slots = {0: block}
    for bit in reversed(bits_of(axis)):
        slots.update({slot ^ bit: swap(piece, axis, bit) for slot, piece in slots.items()})
    return [slots[slot] for slot in range(len(slots))]


def dot(a, b):
    return jnp.dot(a, b, preferred_element_type=F32)


def normalize(values, norm_gain):
    return values * lax.rsqrt(jnp.mean(values * values, axis=-1, keepdims=True) + 1e-05) * norm_gain


class Steps:
    def __init__(self):
        self.token = None

    def __call__(self, kernel, name, outs, args, scratch=(), aliases=None, out_space=pltpu.VMEM):
        tokens = [] if self.token is None else [self.token]
        count, given = len(outs), len(args)
        held = [(a.shape, a.dtype) for a in args] + list(outs)
        size = sum(math.prod(shape) * jnp.dtype(dtype).itemsize for shape, dtype in held)

        def with_token(*refs):
            inputs, rest = refs[:given], refs[given + len(tokens) :]
            outputs, token_ref, scratches = rest[:count], rest[count], rest[count + 1 :]
            kernel(*inputs, *outputs, *scratches)
            token_ref[...] = jnp.zeros_like(token_ref)

        *results, self.token = pl.pallas_call(
            with_token,
            name=name,
            out_shape=[jax.ShapeDtypeStruct(shape, dtype) for shape, dtype in outs]
            + [jax.ShapeDtypeStruct((8, 128), F32)],
            in_specs=[VMEM] * (given + len(tokens)),
            out_specs=[pl.BlockSpec(memory_space=out_space)] * count + [VMEM],
            scratch_shapes=list(scratch),
            input_output_aliases=aliases or {},
            cost_estimate=pl.CostEstimate(flops=1000, bytes_accessed=1000, transcendentals=0),
            compiler_params=pltpu.CompilerParams(vmem_limit_bytes=size + (6 << 20)),
        )(*args, *tokens)
        return results


def load(array):
    def kernel(array_ref, out_ref, sem):
        copy = pltpu.make_async_copy(array_ref, out_ref, sem)
        copy.start()
        copy.wait()

    return pl.pallas_call(
        kernel,
        name="load",
        out_shape=pltpu.VMEM(array.shape, array.dtype),
        in_specs=[pl.BlockSpec(memory_space=pltpu.HBM)],
        out_specs=VMEM,
        scratch_shapes=[pltpu.SemaphoreType.DMA],
        cost_estimate=pl.CostEstimate(flops=1000, bytes_accessed=1 << 24, transcendentals=0),
        compiler_params=pltpu.CompilerParams(vmem_limit_bytes=math.prod(array.shape) * 2 + (6 << 20)),
    )(array)


def row_blocks(rows):
    size = min(rows, 128)
    return [pl.ds(start, size) for start in range(0, rows, size)]


def proj_kernel(start, *refs):
    *piece_refs, weight_ref, out_ref, rows_ref = refs
    code = lax.axis_index("codebook")
    size = rows_ref.shape[0] // len(piece_refs)
    for i in range(len(piece_refs)):
        for slot, piece_ref in enumerate(piece_refs):

            @pl.when(code ^ i == slot)
            def _():
                rows_ref[i * size : (i + 1) * size, :] = piece_ref[start : start + size, :]

    for block in row_blocks(rows_ref.shape[0]):
        out_ref[block, :] = dot(rows_ref[block, :], weight_ref[0])


def embed_kernel(chunk, ids_ref, table_ref, out_ref):
    first = lax.axis_index("codebook") == 0
    start_id = table_ref.shape[1] - 1
    count, length = ids_ref.shape
    size = out_ref.shape[0] // count
    diagonal = lax.broadcasted_iota(jnp.int32, (length, length), 0) == lax.broadcasted_iota(
        jnp.int32, (length, length), 1
    )
    columns = []
    for i in range(count):
        line = ids_ref[i : i + 1, :].astype(F32)
        column = jnp.sum(jnp.where(diagonal, line, 0.0), axis=1, keepdims=True).astype(jnp.int32)
        columns.append(column[chunk * size : (chunk + 1) * size])
    all_ids = jnp.where(first, start_id, jnp.concatenate(columns, axis=0))
    for block in row_blocks(out_ref.shape[0]):
        ids = all_ids[block.start : block.start + block.size]
        token = lax.broadcasted_iota(jnp.int32, (block.size, start_id), 1)
        chosen = (token == ids).astype(F32).astype(BF16)
        started = jnp.where(ids == start_id, 1.0, 0.0) * table_ref[0, start_id:, :].astype(F32)
        out_ref[block, :] = (dot(chosen, table_ref[0, :start_id, :]) + started).astype(BF16)


def sum_kernel(*refs):
    *term_refs, wide_ref, sent_ref = refs
    total = term_refs[0][...].astype(F32)
    for term_ref in term_refs[1:]:
        total = total + term_ref[...].astype(F32)
    wide_ref[...] = total
    sent_ref[...] = total.astype(BF16)


def pass_kernel(given_ref, taken_ref):
    pass


def mix_kernel(terms, *refs):
    outs = 2 if terms else 1
    sent_ref = refs[-1]
    part_refs, term_refs = refs[: len(refs) - outs - terms], refs[len(refs) - outs - terms : -outs]

    def send_part():
        sent_ref[...] = part_refs[0][...].astype(BF16)

    def send_rows():
        total = term_refs[0][...].astype(F32)
        for term_ref in term_refs[1:]:
            total = total + term_ref[...].astype(F32)
        refs[-2][...] = total
        sent_ref[...] = total.astype(BF16)

    if not term_refs:
        send_part()
    elif not part_refs:
        send_rows()
    else:
        pl.when(is_middle())(send_rows)
        pl.when(jnp.logical_not(is_middle()))(send_part)


def choose(wide_ref, arrived_ref, block):
    return jnp.where(is_middle(), wide_ref[block, :], arrived_ref[block, :].astype(F32))


def qkv_kernel(wide_ref, arrived_ref, gain_ref, weight_ref, query_ref, kv_ref):
    for block in row_blocks(wide_ref.shape[0]):
        rows = choose(wide_ref, arrived_ref, block)
        normed = normalize(rows, gain_ref[0, 0:1, :]).astype(BF16)
        query_ref[block, :] = dot(normed, weight_ref[0, 0]).astype(BF16)
        kv_ref[0, block, :] = dot(normed, weight_ref[0, 1]).astype(BF16)
        kv_ref[1, block, :] = dot(normed, weight_ref[0, 2]).astype(BF16)


def per_head(width, lanes, head_size):
    column = lax.broadcasted_iota(jnp.int32, (width, lanes), 0) // head_size
    head = lax.broadcasted_iota(jnp.int32, (width, lanes), 1)
    return (column == head).astype(F32).astype(BF16)


def score(slot, head_size, query, keys):
    product = query * keys.astype(F32)
    high = product.astype(BF16)
    low = (product - high.astype(F32)).astype(BF16)
    gather = per_head(query.shape[1], 128, head_size)
    result = (dot(high, gather) + dot(low, gather)) * head_size ** (-0.5)
    if slot:
        code = lax.axis_index("codebook")
        result = jnp.where((code ^ slot) <= code, result, -1e30)
    return result


def score_kernel(slots, head_size, query_ref, *refs):
    *kv_refs, scores_ref = refs
    for block in row_blocks(query_ref.shape[0]):
        query = query_ref[block, :].astype(F32)
        for i, (slot, kv_ref) in enumerate(zip(slots, kv_refs)):
            scores_ref[i, block, :] = score(slot, head_size, query, kv_ref[0, block, :])


def attend_kernel(early, head_size, query_ref, scores_ref, *refs):
    *kv_refs, weight_ref, part_ref = refs
    width = query_ref.shape[-1]
    lanes = 128
    head_t = lax.broadcasted_iota(jnp.int32, (lanes, width), 0)
    column_t = lax.broadcasted_iota(jnp.int32, (lanes, width), 1) // head_size
    spread = (column_t == head_t).astype(F32).astype(BF16)
    for block in row_blocks(query_ref.shape[0]):
        query = query_ref[block, :].astype(F32)
        scores = []
        for slot, kv_ref in enumerate(kv_refs):
            if slot in early:
                scores.append(scores_ref[early.index(slot), block, :])
            else:
                scores.append(score(slot, head_size, query, kv_ref[0, block, :]))
        highest = functools.reduce(jnp.maximum, scores)
        weights = [jnp.exp(one - highest) for one in scores]
        running = functools.reduce(jnp.add, weights)
        summed = None
        for kv_ref, weight in zip(kv_refs, weights):
            term = dot(weight.astype(BF16), spread) * kv_ref[1, block, :].astype(F32)
            summed = term if summed is None else summed + term
        inverse = 1.0 / running
        high = inverse.astype(BF16)
        low = (inverse - high.astype(F32)).astype(BF16)
        attended = (summed * (dot(high, spread) + dot(low, spread))).astype(BF16)
        part_ref[block, :] = dot(attended, weight_ref[0]).astype(part_ref.dtype)


def mlp_kernel(count, form, wide_ref, arrived_ref, gain_ref, gate_up_ref, down_ref, *refs):
    kept_ref, *sent_refs, act_ref = refs
    sent_ref = sent_refs[0]
    index = lax.axis_index("hidden")
    hidden = act_ref.shape[1]
    step = min(hidden, 256)
    width = down_ref.shape[2] // count
    own = pl.ds(pl.multiple_of(index * width, width), width)
    for block in row_blocks(wide_ref.shape[0]):
        normed = normalize(choose(wide_ref, arrived_ref, block), gain_ref[0, 1:2, :]).astype(BF16)
        residual = jnp.where(is_middle(), wide_ref[block, own], arrived_ref[block, own].astype(F32))
        for start in range(0, hidden, step):
            columns = pl.ds(start, step)
            gate_sum = dot(normed, gate_up_ref[0, 0, :, columns])
            upper_sum = dot(normed, gate_up_ref[0, 1, :, columns])
            act_ref[:, columns] = (jax.nn.silu(gate_sum) * upper_sum).astype(BF16)
        if form == "direct":
            for i in reversed(range(count)):
                owner = index ^ i
                columns = pl.ds(pl.multiple_of(owner * width, width), width)
                total = dot(act_ref[...], down_ref[0, :, columns])
                if i:
                    sent_refs[i - 1][block, :] = total.astype(BF16)
                else:
                    kept_ref[block, :] = total + residual
            continue
        if form == "whole":
            total = dot(act_ref[...], down_ref[0])
            sent_ref[block, :] = total.astype(BF16)
            kept_ref[block, :] = total
            kept_ref[block, own] = kept_ref[block, own] + residual
            sent_refs[1][block, :] = kept_ref[block, own]
            continue
        for i in range(count // 2):
            owner = index ^ (2 * i)
            columns = pl.ds(pl.multiple_of((owner ^ 1) * width, width), width)
            sent_ref[i, block, :] = dot(act_ref[...], down_ref[0, :, columns]).astype(BF16)
        for i in range(count // 2):
            owner = index ^ (2 * i)
            columns = pl.ds(pl.multiple_of(owner * width, width), width)
            total = dot(act_ref[...], down_ref[0, :, columns])
            if i == 0:
                total = total + residual
            kept_ref[i, block, :] = total


def gather_kernel(mine_ref, arrived_ref, wide_ref, sent_ref):
    index = lax.axis_index("hidden")
    width = wide_ref.shape[2]
    far = lax.axis_size("hidden") - 1 - index

    def columns(owner):
        return pl.ds(pl.multiple_of(owner * width, width), width)

    def total(owner):
        return mine_ref[:, columns(owner)] + arrived_ref[:, columns(owner)].astype(F32)

    wide_ref[0] = total(index)
    wide_ref[1] = mine_ref[:, columns(index ^ 1)]
    sent_ref[0] = total(far).astype(BF16)
    sent_ref[1] = total(far ^ 1).astype(BF16)


def return_kernel(wide_ref, arrived_ref, own_ref, sent_ref):
    own_ref[...] = wide_ref[0] + arrived_ref[0].astype(F32)
    sent_ref[...] = (wide_ref[1] + arrived_ref[1].astype(F32)).astype(BF16)


def halve_kernel(mine_ref, arrived_ref, wide_ref, sent_ref):
    kept = wide_ref.shape[0]
    wide_ref[...] = mine_ref[:kept] + arrived_ref[:kept].astype(F32)
    sent_ref[...] = (mine_ref[kept:] + arrived_ref[kept:].astype(F32)).astype(BF16)


def final_kernel(forms, *refs):
    *in_refs, out_ref, rows_ref, sems = refs
    chunks, count, size, width = rows_ref.shape
    shape = (count, size, width)
    copies = []
    for chunk in range(chunks):
        if forms[chunk] == "direct":
            total_ref, *in_refs = in_refs
            total = total_ref[...]
            for arrived_ref in in_refs:
                total = total + arrived_ref[...].astype(F32)
            rows_ref[chunk] = total.reshape(shape)
        elif forms[chunk] == "whole":
            own_ref, mine_ref, arrived_ref, *in_refs = in_refs

            @pl.when(is_middle())
            def _():
                rows_ref[chunk] = own_ref[...].reshape(shape)

            @pl.when(jnp.logical_not(is_middle()))
            def _():
                rows_ref[chunk] = (mine_ref[...] + arrived_ref[...].astype(F32)).reshape(shape)

        else:
            wide_ref, arrived_ref, *in_refs = in_refs
            rows_ref[chunk] = (wide_ref[0] + arrived_ref[0].astype(F32)).reshape(shape)
        target = out_ref.at[0, :, pl.ds(chunk * size, size), :]
        copies.append(pltpu.make_async_copy(rows_ref.at[chunk], target, sems.at[chunk]))
        copies[-1].start()
    for copy in copies:
        copy.wait()


def body(
    temporal,
    frame_ids,
    proj_weight,
    embed_table,
    qkv_weight,
    out_weight,
    gate_up,
    down_weight,
    norm_gains,
):
    hidden_count = lax.axis_size("hidden")
    code_count = lax.axis_size("codebook")
    pair_bit, far_bit = bits_of("hidden")
    code_bits = bits_of("codebook")[::-1]
    width = embed_table.shape[2]
    local_width = qkv_weight.shape[3]
    head_size = width // HEADS

    block_rows = temporal.shape[0]
    size = block_rows // CHUNKS
    rows = code_count * size
    row_count = code_count * block_rows
    pieces = [slots_of(part, "codebook") for part in (temporal[:size], temporal[size:])]
    earlier = shifted(frame_ids.reshape(code_count, -1), "codebook", 1)
    step = Steps()
    wide, sent = ((rows, width), F32), ((rows, width), BF16)
    states = [{} for _ in range(CHUNKS)]

    def get(c):
        return states[c] if 0 <= c < CHUNKS else None

    def project(c):
        if (s := get(c)) is not None:
            s["part"] = step(
                functools.partial(proj_kernel, max(c - 1, 0) * size),
                "project",
                [wide],
                [*pieces[min(c, 1)], proj_weight],
                [pltpu.VMEM((rows, temporal.shape[1]), BF16)],
            )[0]

    def embed(c):
        if (s := get(c)) is not None:
            s["embedded"] = step(
                functools.partial(embed_kernel, c), "embed", [sent], [earlier, embed_table]
            )[0]

    def exchange(t):
        giver = get(t) if get(t) is not None else get(t - 4)
        name = "part"
        if giver is None and get(t - 8) is not None and get(t - 6) is not None:
            giver, name = get(t - 8), "sums_sent"
        early = get(t - 2)
        taker = early if early is not None else get(t - 6)
        if giver is None and taker is None:
            return
        names = ["total", "far", "embedded"] if early is not None else ["x_zero", "total", "far"]
        parts = [giver[name]] if giver is not None else []
        terms = [taker[name] for name in names] if taker is not None else []
        *finished, out = step(
            functools.partial(mix_kernel, len(terms)),
            "exchange",
            [wide, sent] if terms else [sent],
            [*parts, *terms],
        )
        arrived = swap(out, "hidden", pair_bit)
        if giver is not None:
            giver["arrived"] = arrived
        if taker is not None:
            done = "x_zero" if early is not None else "residual"
            taker[done], taker[done + "_arrived"] = finished[0], arrived

    def pair_sum(c):
        if (s := get(c)) is not None:
            s["total"], out = step(sum_kernel, "pair_sum", [wide, sent], [s["part"], s["arrived"]])
            s["far"] = middle_swap(out)

    def qkv(c):
        if (s := get(c)) is not None:
            s["query"], kv = step(
                qkv_kernel,
                "qkv",
                [((rows, local_width), BF16), ((2, rows, local_width), BF16)],
                [s["x_zero"], s["x_zero_arrived"], norm_gains, qkv_weight],
            )
            s["kvs"] = {0: kv} | {bit: swap(kv, "codebook", bit) for bit in code_bits}

    def forward(c):
        if (s := get(c)) is not None:
            for bit in code_bits:
                for slot in [slot for slot in s["kvs"] if slot > bit and not slot & (2 * bit - 1)]:
                    (kv,) = step(pass_kernel, "pass", [((2, rows, local_width), BF16)], [s["kvs"][slot]], aliases={0: 0})
                    s["kvs"][slot], s["kvs"][slot ^ bit] = kv, swap(kv, "codebook", bit)

    def attend(c):
        if (s := get(c)) is not None:
            early = (0, *code_bits)
            (scores,) = step(
                functools.partial(score_kernel, early, head_size),
                "score",
                [((len(early), rows, 128), F32)],
                [s["query"], *[s["kvs"][slot] for slot in early]],
            )
            s["part"] = step(
                functools.partial(attend_kernel, early, head_size),
                "attend",
                [wide],
                [s["query"], scores, *[s["kvs"][slot] for slot in range(code_count)], out_weight],
            )[0]

    def form(c):
        if c + 8 < CHUNKS + 6:
            return "whole"
        return "direct" if c == CHUNKS - 1 else "halves"

    def mlp(c):
        if (s := get(c)) is not None:
            shape = {
                "whole": (rows, width),
                "halves": (hidden_count // 2, rows, local_width),
                "direct": (rows, local_width),
            }[form(c)]
            more = {"whole": [F32], "halves": [], "direct": [BF16] * (hidden_count - 2)}[form(c)]
            s["sums"], s["sums_sent"], *others = step(
                functools.partial(mlp_kernel, hidden_count, form(c)),
                "mlp",
                [(shape, F32), (shape, BF16)] + [((rows, local_width), dtype) for dtype in more],
                [s["residual"], s["residual_arrived"], norm_gains, gate_up, down_weight],
                [pltpu.VMEM((min(rows, 128), gate_up.shape[3]), BF16)],
            )
            if form(c) == "whole":
                s["mine"] = others[0]
            if form(c) == "halves":
                s["arrived"] = swap(s["sums_sent"], "hidden", pair_bit)
            if form(c) == "direct":
                others = [s["sums_sent"], *others]
                s["direct"] = [swap(out, "hidden", i + 1) for i, out in reversed(list(enumerate(others)))]

    def halve(c):
        if (s := get(c)) is not None and form(c) == "halves":
            shape = (hidden_count // 4, rows, local_width)
            s["wide"], out = step(
                halve_kernel, "halve", [(shape, F32), (shape, BF16)], [s["sums"], s["arrived"]]
            )
            s["last"] = swap(out, "hidden", far_bit)

    def collect(c):
        if (s := get(c)) is not None and form(c) == "whole":
            shape = (2, rows, local_width)
            s["wide"], out = step(
                gather_kernel, "gather", [(shape, F32), (shape, BF16)], [s["sums"], s["arrived"]]
            )
            s["far"] = middle_swap(out)

    def give_back(c):
        if (s := get(c)) is not None and form(c) == "whole":
            shape = (rows, local_width)
            s["own"], out = step(
                return_kernel, "return", [(shape, F32), (shape, BF16)], [s["wide"], s["far"]]
            )
            s["last"] = swap(out, "hidden", pair_bit)

    def final():
        forms = [form(c) for c in range(CHUNKS)]
        args = []
        for s, kind in zip(states, forms):
            names = {"whole": ("own", "mine", "last"), "halves": ("wide", "last"), "direct": ("sums",)}[kind]
            args += [s[name] for name in names] + s.get("direct", [])
        out = step(
            functools.partial(final_kernel, forms),
            "final",
            [((1, code_count, block_rows, local_width), F32)],
            args,
            [
                pltpu.VMEM((CHUNKS, code_count, size, local_width), F32),
                pltpu.SemaphoreType.DMA((CHUNKS,)),
            ],
            out_space=pl.ANY,
        )[0]
        return out.reshape(1, row_count, local_width)

    stages = 9
    project(0)
    for t in range(CHUNKS + stages - 1):
        if t < 3:
            exchange(t)
            pair_sum(t - 1)
        else:
            pair_sum(t - 1)
            pair_sum(t - 5)
            qkv(t - 3)
            exchange(t)
        collect(t - 9)
        mlp(t - 7)
        give_back(t - 10)
        halve(t - 8)
        project(t + 1)
        embed(t - 1)
        forward(t - 3)
        attend(t - 3)
    return final()


def solution(mesh):
    placed = (
        P(("frames", "codebook"), "hidden"),
        P("frames", "codebook"),
        P("codebook", "hidden", None),
        P("codebook", None, None),
        P("codebook", None, None, "hidden"),
        P("codebook", "hidden", None),
        P("codebook", None, None, "hidden"),
        P("codebook", "hidden", None),
        P("codebook", None, None),
    )
    return jax.shard_map(
        body,
        mesh=mesh,
        in_specs=placed,
        out_specs=P("codebook", "frames", "hidden"),
        check_vma=False,
    )
```

```python
import functools
import math

import jax
import jax.numpy as jnp
from jax import lax
from jax.experimental import pallas as pl
from jax.experimental.pallas import tpu as pltpu
from jax.sharding import PartitionSpec as P

HEADS = 16
CHUNKS = 4
F32 = jnp.float32
BF16 = jnp.bfloat16
VMEM = pl.BlockSpec(memory_space=pltpu.VMEM)


def swap(block, axis, distance):
    count = lax.axis_size(axis)
    return lax.ppermute(block, axis, [(i, i ^ distance) for i in range(count)])


def middle_swap(block):
    ends, codes = lax.axis_size("hidden"), lax.axis_size("codebook")
    route = []
    for code in range(codes):
        for i in range(ends):
            other = (code, ends - 1 - i) if 0 < i < ends - 1 else (code ^ 1, i)
            route.append((code * ends + i, other[0] * ends + other[1]))
    return lax.ppermute(block, ("codebook", "hidden"), route)


def is_middle():
    index = lax.axis_index("hidden")
    return (index > 0) & (index < lax.axis_size("hidden") - 1)


def bits_of(axis):
    count = lax.axis_size(axis)
    return [1 << b for b in range(count.bit_length() - 1)]


def shifted(block, axis, distance):
    devices = range(lax.axis_size(axis))
    route = [(i - distance, i) for i in devices if i - distance in devices]
    return lax.ppermute(block, axis, route)


def slots_of(block, axis):
    slots = {0: block}
    for bit in reversed(bits_of(axis)):
        slots.update({slot ^ bit: swap(piece, axis, bit) for slot, piece in slots.items()})
    return [slots[slot] for slot in range(len(slots))]


def dot(a, b):
    return jnp.dot(a, b, preferred_element_type=F32)


def normalize(values, norm_gain):
    return values * lax.rsqrt(jnp.mean(values * values, axis=-1, keepdims=True) + 1e-05) * norm_gain


class Steps:
    def __init__(self):
        self.token = None

    def __call__(self, kernel, name, outs, args, scratch=(), aliases=None, out_space=pltpu.VMEM):
        tokens = [] if self.token is None else [self.token]
        count, given = len(outs), len(args)
        held = [(a.shape, a.dtype) for a in args] + list(outs)
        size = sum(math.prod(shape) * jnp.dtype(dtype).itemsize for shape, dtype in held)

        def with_token(*refs):
            inputs, rest = refs[:given], refs[given + len(tokens) :]
            outputs, token_ref, scratches = rest[:count], rest[count], rest[count + 1 :]
            kernel(*inputs, *outputs, *scratches)
            token_ref[...] = jnp.zeros_like(token_ref)

        *results, self.token = pl.pallas_call(
            with_token,
            name=name,
            out_shape=[jax.ShapeDtypeStruct(shape, dtype) for shape, dtype in outs]
            + [jax.ShapeDtypeStruct((8, 128), F32)],
            in_specs=[VMEM] * (given + len(tokens)),
            out_specs=[pl.BlockSpec(memory_space=out_space)] * count + [VMEM],
            scratch_shapes=list(scratch),
            input_output_aliases=aliases or {},
            cost_estimate=pl.CostEstimate(flops=1000, bytes_accessed=1000, transcendentals=0),
            compiler_params=pltpu.CompilerParams(vmem_limit_bytes=size + (6 << 20)),
        )(*args, *tokens)
        return results


def load(array):
    def kernel(array_ref, out_ref, sem):
        copy = pltpu.make_async_copy(array_ref, out_ref, sem)
        copy.start()
        copy.wait()

    return pl.pallas_call(
        kernel,
        name="load",
        out_shape=pltpu.VMEM(array.shape, array.dtype),
        in_specs=[pl.BlockSpec(memory_space=pltpu.HBM)],
        out_specs=VMEM,
        scratch_shapes=[pltpu.SemaphoreType.DMA],
        cost_estimate=pl.CostEstimate(flops=1000, bytes_accessed=1 << 24, transcendentals=0),
        compiler_params=pltpu.CompilerParams(vmem_limit_bytes=math.prod(array.shape) * 2 + (6 << 20)),
    )(array)


def row_blocks(rows):
    size = min(rows, 128)
    return [pl.ds(start, size) for start in range(0, rows, size)]


def proj_kernel(start, *refs):
    *piece_refs, weight_ref, out_ref, rows_ref = refs
    code = lax.axis_index("codebook")
    size = rows_ref.shape[0] // len(piece_refs)
    for i in range(len(piece_refs)):
        for slot, piece_ref in enumerate(piece_refs):

            @pl.when(code ^ i == slot)
            def _():
                rows_ref[i * size : (i + 1) * size, :] = piece_ref[start : start + size, :]

    for block in row_blocks(rows_ref.shape[0]):
        out_ref[block, :] = dot(rows_ref[block, :], weight_ref[0])


def embed_kernel(chunk, ids_ref, table_ref, out_ref):
    first = lax.axis_index("codebook") == 0
    start_id = table_ref.shape[1] - 1
    count, length = ids_ref.shape
    size = out_ref.shape[0] // count
    diagonal = lax.broadcasted_iota(jnp.int32, (length, length), 0) == lax.broadcasted_iota(
        jnp.int32, (length, length), 1
    )
    columns = []
    for i in range(count):
        line = ids_ref[i : i + 1, :].astype(F32)
        column = jnp.sum(jnp.where(diagonal, line, 0.0), axis=1, keepdims=True).astype(jnp.int32)
        columns.append(column[chunk * size : (chunk + 1) * size])
    all_ids = jnp.where(first, start_id, jnp.concatenate(columns, axis=0))
    for block in row_blocks(out_ref.shape[0]):
        ids = all_ids[block.start : block.start + block.size]
        token = lax.broadcasted_iota(jnp.int32, (block.size, start_id), 1)
        chosen = (token == ids).astype(F32).astype(BF16)
        started = jnp.where(ids == start_id, 1.0, 0.0) * table_ref[0, start_id:, :].astype(F32)
        out_ref[block, :] = (dot(chosen, table_ref[0, :start_id, :]) + started).astype(BF16)


def sum_kernel(*refs):
    *term_refs, wide_ref, sent_ref = refs
    total = term_refs[0][...].astype(F32)
    for term_ref in term_refs[1:]:
        total = total + term_ref[...].astype(F32)
    wide_ref[...] = total
    sent_ref[...] = total.astype(BF16)


def pass_kernel(given_ref, taken_ref):
    pass


def mix_kernel(terms, *refs):
    outs = 2 if terms else 1
    sent_ref = refs[-1]
    part_refs, term_refs = refs[: len(refs) - outs - terms], refs[len(refs) - outs - terms : -outs]

    def send_part():
        sent_ref[...] = part_refs[0][...].astype(BF16)

    def send_rows():
        total = term_refs[0][...].astype(F32)
        for term_ref in term_refs[1:]:
            total = total + term_ref[...].astype(F32)
        refs[-2][...] = total
        sent_ref[...] = total.astype(BF16)

    if not term_refs:
        send_part()
    elif not part_refs:
        send_rows()
    else:
        pl.when(is_middle())(send_rows)
        pl.when(jnp.logical_not(is_middle()))(send_part)


def choose(wide_ref, arrived_ref, block):
    return jnp.where(is_middle(), wide_ref[block, :], arrived_ref[block, :].astype(F32))


def qkv_kernel(wide_ref, arrived_ref, gain_ref, weight_ref, query_ref, kv_ref):
    for block in row_blocks(wide_ref.shape[0]):
        rows = choose(wide_ref, arrived_ref, block)
        normed = normalize(rows, gain_ref[0, 0:1, :]).astype(BF16)
        query_ref[block, :] = dot(normed, weight_ref[0, 0]).astype(BF16)
        kv_ref[0, block, :] = dot(normed, weight_ref[0, 1]).astype(BF16)
        kv_ref[1, block, :] = dot(normed, weight_ref[0, 2]).astype(BF16)


def per_head(width, lanes, head_size):
    column = lax.broadcasted_iota(jnp.int32, (width, lanes), 0) // head_size
    head = lax.broadcasted_iota(jnp.int32, (width, lanes), 1)
    return (column == head).astype(F32).astype(BF16)


def score(slot, head_size, query, keys):
    product = query * keys.astype(F32)
    high = product.astype(BF16)
    low = (product - high.astype(F32)).astype(BF16)
    gather = per_head(query.shape[1], 128, head_size)
    result = (dot(high, gather) + dot(low, gather)) * head_size ** (-0.5)
    if slot:
        code = lax.axis_index("codebook")
        result = jnp.where((code ^ slot) <= code, result, -1e30)
    return result


def score_kernel(slots, head_size, query_ref, *refs):
    *kv_refs, scores_ref = refs
    for block in row_blocks(query_ref.shape[0]):
        query = query_ref[block, :].astype(F32)
        for i, (slot, kv_ref) in enumerate(zip(slots, kv_refs)):
            scores_ref[i, block, :] = score(slot, head_size, query, kv_ref[0, block, :])


def attend_kernel(early, head_size, query_ref, scores_ref, *refs):
    *kv_refs, weight_ref, part_ref = refs
    width = query_ref.shape[-1]
    lanes = 128
    head_t = lax.broadcasted_iota(jnp.int32, (lanes, width), 0)
    column_t = lax.broadcasted_iota(jnp.int32, (lanes, width), 1) // head_size
    spread = (column_t == head_t).astype(F32).astype(BF16)
    for block in row_blocks(query_ref.shape[0]):
        query = query_ref[block, :].astype(F32)
        scores = []
        for slot, kv_ref in enumerate(kv_refs):
            if slot in early:
                scores.append(scores_ref[early.index(slot), block, :])
            else:
                scores.append(score(slot, head_size, query, kv_ref[0, block, :]))
        highest = functools.reduce(jnp.maximum, scores)
        weights = [jnp.exp(one - highest) for one in scores]
        running = functools.reduce(jnp.add, weights)
        summed = None
        for kv_ref, weight in zip(kv_refs, weights):
            term = dot(weight.astype(BF16), spread) * kv_ref[1, block, :].astype(F32)
            summed = term if summed is None else summed + term
        inverse = 1.0 / running
        high = inverse.astype(BF16)
        low = (inverse - high.astype(F32)).astype(BF16)
        attended = (summed * (dot(high, spread) + dot(low, spread))).astype(BF16)
        part_ref[block, :] = dot(attended, weight_ref[0]).astype(part_ref.dtype)


def mlp_kernel(count, form, wide_ref, arrived_ref, gain_ref, gate_up_ref, down_ref, *refs):
    kept_ref, *sent_refs, act_ref = refs
    sent_ref = sent_refs[0]
    index = lax.axis_index("hidden")
    hidden = act_ref.shape[1]
    step = min(hidden, 256)
    width = down_ref.shape[2] // count
    own = pl.ds(pl.multiple_of(index * width, width), width)
    for block in row_blocks(wide_ref.shape[0]):
        normed = normalize(choose(wide_ref, arrived_ref, block), gain_ref[0, 1:2, :]).astype(BF16)
        residual = jnp.where(is_middle(), wide_ref[block, own], arrived_ref[block, own].astype(F32))
        for start in range(0, hidden, step):
            columns = pl.ds(start, step)
            gate_sum = dot(normed, gate_up_ref[0, 0, :, columns])
            upper_sum = dot(normed, gate_up_ref[0, 1, :, columns])
            act_ref[:, columns] = (jax.nn.silu(gate_sum) * upper_sum).astype(BF16)
        if form == "direct":
            for i in reversed(range(count)):
                owner = index ^ i
                columns = pl.ds(pl.multiple_of(owner * width, width), width)
                total = dot(act_ref[...], down_ref[0, :, columns])
                if i:
                    sent_refs[i - 1][block, :] = total.astype(BF16)
                else:
                    kept_ref[block, :] = total + residual
            continue
        if form == "whole":
            total = dot(act_ref[...], down_ref[0])
            sent_ref[block, :] = total.astype(BF16)
            kept_ref[block, :] = total
            kept_ref[block, own] = kept_ref[block, own] + residual
            sent_refs[1][block, :] = kept_ref[block, own]
            continue
        for i in range(count // 2):
            owner = index ^ (2 * i)
            columns = pl.ds(pl.multiple_of((owner ^ 1) * width, width), width)
            sent_ref[i, block, :] = dot(act_ref[...], down_ref[0, :, columns]).astype(BF16)
        for i in range(count // 2):
            owner = index ^ (2 * i)
            columns = pl.ds(pl.multiple_of(owner * width, width), width)
            total = dot(act_ref[...], down_ref[0, :, columns])
            if i == 0:
                total = total + residual
            kept_ref[i, block, :] = total


def gather_kernel(mine_ref, arrived_ref, wide_ref, sent_ref):
    index = lax.axis_index("hidden")
    width = wide_ref.shape[2]
    far = lax.axis_size("hidden") - 1 - index

    def columns(owner):
        return pl.ds(pl.multiple_of(owner * width, width), width)

    def total(owner):
        return mine_ref[:, columns(owner)] + arrived_ref[:, columns(owner)].astype(F32)

    wide_ref[0] = total(index)
    wide_ref[1] = mine_ref[:, columns(index ^ 1)]
    sent_ref[0] = total(far).astype(BF16)
    sent_ref[1] = total(far ^ 1).astype(BF16)


def return_kernel(wide_ref, arrived_ref, own_ref, sent_ref):
    own_ref[...] = wide_ref[0] + arrived_ref[0].astype(F32)
    sent_ref[...] = (wide_ref[1] + arrived_ref[1].astype(F32)).astype(BF16)


def halve_kernel(mine_ref, arrived_ref, wide_ref, sent_ref):
    kept = wide_ref.shape[0]
    wide_ref[...] = mine_ref[:kept] + arrived_ref[:kept].astype(F32)
    sent_ref[...] = (mine_ref[kept:] + arrived_ref[kept:].astype(F32)).astype(BF16)


def final_kernel(forms, *refs):
    *in_refs, out_ref, rows_ref, sems = refs
    chunks, count, size, width = rows_ref.shape
    shape = (count, size, width)
    copies = []
    for chunk in range(chunks):
        if forms[chunk] == "direct":
            total_ref, *in_refs = in_refs
            total = total_ref[...]
            for arrived_ref in in_refs:
                total = total + arrived_ref[...].astype(F32)
            rows_ref[chunk] = total.reshape(shape)
        elif forms[chunk] == "whole":
            own_ref, mine_ref, arrived_ref, *in_refs = in_refs

            @pl.when(is_middle())
            def _():
                rows_ref[chunk] = own_ref[...].reshape(shape)

            @pl.when(jnp.logical_not(is_middle()))
            def _():
                rows_ref[chunk] = (mine_ref[...] + arrived_ref[...].astype(F32)).reshape(shape)

        else:
            wide_ref, arrived_ref, *in_refs = in_refs
            rows_ref[chunk] = (wide_ref[0] + arrived_ref[0].astype(F32)).reshape(shape)
        target = out_ref.at[0, :, pl.ds(chunk * size, size), :]
        copies.append(pltpu.make_async_copy(rows_ref.at[chunk], target, sems.at[chunk]))
        copies[-1].start()
    for copy in copies:
        copy.wait()


def body(
    temporal,
    frame_ids,
    proj_weight,
    embed_table,
    qkv_weight,
    out_weight,
    gate_up,
    down_weight,
    norm_gains,
):
    hidden_count = lax.axis_size("hidden")
    code_count = lax.axis_size("codebook")
    pair_bit, far_bit = bits_of("hidden")
    code_bits = bits_of("codebook")[::-1]
    width = embed_table.shape[2]
    local_width = qkv_weight.shape[3]
    head_size = width // HEADS

    block_rows = temporal.shape[0]
    size = block_rows // CHUNKS
    rows = code_count * size
    row_count = code_count * block_rows
    pieces = [slots_of(part, "codebook") for part in (temporal[:size], temporal[size:])]
    earlier = shifted(frame_ids.reshape(code_count, -1), "codebook", 1)
    step = Steps()
    wide, sent = ((rows, width), F32), ((rows, width), BF16)
    states = [{} for _ in range(CHUNKS)]

    def get(c):
        return states[c] if 0 <= c < CHUNKS else None

    def project(c):
        if (s := get(c)) is not None:
            s["part"] = step(
                functools.partial(proj_kernel, max(c - 1, 0) * size),
                "project",
                [wide],
                [*pieces[min(c, 1)], proj_weight],
                [pltpu.VMEM((rows, temporal.shape[1]), BF16)],
            )[0]

    def embed(c):
        if (s := get(c)) is not None:
            s["embedded"] = step(
                functools.partial(embed_kernel, c), "embed", [sent], [earlier, embed_table]
            )[0]

    def exchange(t):
        giver = get(t) if get(t) is not None else get(t - 4)
        name = "part"
        if giver is None and get(t - 8) is not None and get(t - 6) is not None:
            giver, name = get(t - 8), "sums_sent"
        early = get(t - 2)
        taker = early if early is not None else get(t - 6)
        if giver is None and taker is None:
            return
        names = ["total", "far", "embedded"] if early is not None else ["x_zero", "total", "far"]
        parts = [giver[name]] if giver is not None else []
        terms = [taker[name] for name in names] if taker is not None else []
        *finished, out = step(
            functools.partial(mix_kernel, len(terms)),
            "exchange",
            [wide, sent] if terms else [sent],
            [*parts, *terms],
        )
        arrived = swap(out, "hidden", pair_bit)
        if giver is not None:
            giver["arrived"] = arrived
        if taker is not None:
            done = "x_zero" if early is not None else "residual"
            taker[done], taker[done + "_arrived"] = finished[0], arrived

    def pair_sum(c):
        if (s := get(c)) is not None:
            s["total"], out = step(sum_kernel, "pair_sum", [wide, sent], [s["part"], s["arrived"]])
            s["far"] = middle_swap(out)

    def qkv(c):
        if (s := get(c)) is not None:
            s["query"], kv = step(
                qkv_kernel,
                "qkv",
                [((rows, local_width), BF16), ((2, rows, local_width), BF16)],
                [s["x_zero"], s["x_zero_arrived"], norm_gains, qkv_weight],
            )
            s["kvs"] = {0: kv} | {bit: swap(kv, "codebook", bit) for bit in code_bits}

    def forward(c):
        if (s := get(c)) is not None:
            for bit in code_bits:
                for slot in [slot for slot in s["kvs"] if slot > bit and not slot & (2 * bit - 1)]:
                    (kv,) = step(pass_kernel, "pass", [((2, rows, local_width), BF16)], [s["kvs"][slot]], aliases={0: 0})
                    s["kvs"][slot], s["kvs"][slot ^ bit] = kv, swap(kv, "codebook", bit)

    def attend(c):
        if (s := get(c)) is not None:
            early = (0, *code_bits)
            (scores,) = step(
                functools.partial(score_kernel, early, head_size),
                "score",
                [((len(early), rows, 128), F32)],
                [s["query"], *[s["kvs"][slot] for slot in early]],
            )
            s["part"] = step(
                functools.partial(attend_kernel, early, head_size),
                "attend",
                [wide],
                [s["query"], scores, *[s["kvs"][slot] for slot in range(code_count)], out_weight],
            )[0]

    def form(c):
        if c + 8 < CHUNKS + 6:
            return "whole"
        return "direct" if c == CHUNKS - 1 else "halves"

    def mlp(c):
        if (s := get(c)) is not None:
            shape = {
                "whole": (rows, width),
                "halves": (hidden_count // 2, rows, local_width),
                "direct": (rows, local_width),
            }[form(c)]
            more = {"whole": [F32], "halves": [], "direct": [BF16] * (hidden_count - 2)}[form(c)]
            s["sums"], s["sums_sent"], *others = step(
                functools.partial(mlp_kernel, hidden_count, form(c)),
                "mlp",
                [(shape, F32), (shape, BF16)] + [((rows, local_width), dtype) for dtype in more],
                [s["residual"], s["residual_arrived"], norm_gains, gate_up, down_weight],
                [pltpu.VMEM((min(rows, 128), gate_up.shape[3]), BF16)],
            )
            if form(c) == "whole":
                s["mine"] = others[0]
            if form(c) == "halves":
                s["arrived"] = swap(s["sums_sent"], "hidden", pair_bit)
            if form(c) == "direct":
                others = [s["sums_sent"], *others]
                s["direct"] = [swap(out, "hidden", i + 1) for i, out in reversed(list(enumerate(others)))]

    def halve(c):
        if (s := get(c)) is not None and form(c) == "halves":
            shape = (hidden_count // 4, rows, local_width)
            s["wide"], out = step(
                halve_kernel, "halve", [(shape, F32), (shape, BF16)], [s["sums"], s["arrived"]]
            )
            s["last"] = swap(out, "hidden", far_bit)

    def collect(c):
        if (s := get(c)) is not None and form(c) == "whole":
            shape = (2, rows, local_width)
            s["wide"], out = step(
                gather_kernel, "gather", [(shape, F32), (shape, BF16)], [s["sums"], s["arrived"]]
            )
            s["far"] = middle_swap(out)

    def give_back(c):
        if (s := get(c)) is not None and form(c) == "whole":
            shape = (rows, local_width)
            s["own"], out = step(
                return_kernel, "return", [(shape, F32), (shape, BF16)], [s["wide"], s["far"]]
            )
            s["last"] = swap(out, "hidden", pair_bit)

    def final():
        forms = [form(c) for c in range(CHUNKS)]
        args = []
        for s, kind in zip(states, forms):
            names = {"whole": ("own", "mine", "last"), "halves": ("wide", "last"), "direct": ("sums",)}[kind]
            args += [s[name] for name in names] + s.get("direct", [])
        out = step(
            functools.partial(final_kernel, forms),
            "final",
            [((1, code_count, block_rows, local_width), F32)],
            args,
            [
                pltpu.VMEM((CHUNKS, code_count, size, local_width), F32),
                pltpu.SemaphoreType.DMA((CHUNKS,)),
            ],
            out_space=pl.ANY,
        )[0]
        return out.reshape(1, row_count, local_width)

    stages = 9
    project(0)
    for t in range(CHUNKS + stages - 1):
        if t < 3:
            exchange(t)
            pair_sum(t - 1)
        else:
            pair_sum(t - 1)
            pair_sum(t - 5)
            qkv(t - 3)
            exchange(t)
        collect(t - 9)
        mlp(t - 7)
        give_back(t - 10)
        halve(t - 8)
        embed(t - 1)
        forward(t - 3)
        project(t + 1)
        attend(t - 3)
    return final()


def solution(mesh):
    placed = (
        P(("frames", "codebook"), "hidden"),
        P("frames", "codebook"),
        P("codebook", "hidden", None),
        P("codebook", None, None),
        P("codebook", None, None, "hidden"),
        P("codebook", "hidden", None),
        P("codebook", None, None, "hidden"),
        P("codebook", "hidden", None),
        P("codebook", None, None),
    )
    return jax.shard_map(
        body,
        mesh=mesh,
        in_specs=placed,
        out_specs=P("codebook", "frames", "hidden"),
        check_vma=False,
    )
```
